128 devices in a mesh: seq: 8 (over z, x_hi), fsdp: 16 (over x_lo, y, core).
Axes of the slice: x: 4 (x_hi: 2, x_lo: 2; x = x_hi * 2 + x_lo), y: 4, z: 4, core: 2. Of those that a mesh axis runs over, the one named last changes fastest.
Arguments:
- middle_state: bfloat16 [16, 4096, 4096], P('fsdp', 'seq'), may hold values from -80 to 80
- newest_state: bfloat16 [16, 4096, 4096], P('fsdp', 'seq'), may hold values from -6 to 6
- middle_cotangent: bfloat16 [16, 4096, 4096], P('fsdp', 'seq'), may hold values from -6 to 6
- newest_cotangent: bfloat16 [16, 4096, 4096], P('fsdp', 'seq'), may hold values from -6 to 6
- log_decay: int32 [16, 4096, 32], P('fsdp', 'seq'), may hold values from -3079 to 0
- state_weights: bfloat16 [4096, 256], P('fsdp'), may hold values from -0.09375 to 0.09375
- skip_gain: float32 [32], replicated, may hold values from 0.5 to 1.5
Outputs:
- rebuilt_oldest: bfloat16 [16, 4096, 4096], P('fsdp', 'seq')
- middle_gradient: bfloat16 [16, 4096, 4096], P('fsdp', 'seq')
- weights_gradient: float32 [4096, 256], P(('seq', 'fsdp'))
The draws below stay inside these ranges and needn't reach their ends.
All inputs are finite; a program needn't handle non-finite values.
Results may differ from the reference program's by a relative error of at most 0.017.
Values may be sent and summed in bfloat16 or wider, within the bound.
A program may use at most 256 MiB of HBM per device.

```python
import jax
import jax.numpy as jnp
from jax import lax

D = 4096
HALF_HEADS = 32
P_SIZE = 128
N = 128
GROUP = 256
TOK_DEV = 512
SEQUENCE_COUNT = 16
SEQUENCE_LENGTH = 4096


def draw_log_decay(key, part):
    random_keys = jax.random.split(jax.random.fold_in(key, 11), 8)
    block_count = SEQUENCE_LENGTH // TOK_DEV
    fast_heads = jax.random.randint(random_keys[0], (SEQUENCE_COUNT, 1, HALF_HEADS), 0, 2)
    base_rate = jax.random.randint(random_keys[1], (SEQUENCE_COUNT, 1, HALF_HEADS), 40, 81)
    block_factor = jax.random.randint(random_keys[2], (SEQUENCE_COUNT, block_count, 1, HALF_HEADS), 2, 5)
    block_factor = jnp.broadcast_to(block_factor, (SEQUENCE_COUNT, block_count, TOK_DEV, HALF_HEADS)).reshape(SEQUENCE_COUNT, SEQUENCE_LENGTH, HALF_HEADS)
    jitter = jax.random.randint(random_keys[3], (SEQUENCE_COUNT, SEQUENCE_LENGTH, HALF_HEADS), 2, 7)
    fast_rate = base_rate * block_factor * jitter // 8
    slow_level = jax.random.randint(random_keys[4], (SEQUENCE_COUNT, block_count, 1, HALF_HEADS), 1, 4)
    slow_level = jnp.broadcast_to(slow_level, (SEQUENCE_COUNT, block_count, TOK_DEV, HALF_HEADS)).reshape(SEQUENCE_COUNT, SEQUENCE_LENGTH, HALF_HEADS)
    slow_pick = jax.random.randint(random_keys[5], (SEQUENCE_COUNT, SEQUENCE_LENGTH, HALF_HEADS), 0, 4)
    slow_rate = jnp.where(slow_pick < slow_level, 1, 0)
    every_rate = jnp.where(fast_heads == 1, fast_rate, slow_rate)
    spike_position = jax.random.randint(random_keys[6], (SEQUENCE_COUNT, 2), 0, SEQUENCE_LENGTH)
    token_positions = jnp.arange(SEQUENCE_LENGTH)
    spike_mask = jnp.any(token_positions[None, :, None] == spike_position[:, None, :], axis=-1)
    spike_scale = jax.random.randint(random_keys[7], (SEQUENCE_COUNT, SEQUENCE_LENGTH, HALF_HEADS), 914, 2840)
    every_rate = every_rate + jnp.where(spike_mask[:, :, None], spike_scale, 0)
    return (-every_rate).astype(jnp.int32)


def draw_middle_state(key, part):
    random_keys = jax.random.split(jax.random.fold_in(key, 23), 3)
    row_scale = jnp.exp(jax.random.uniform(random_keys[0], (SEQUENCE_COUNT, SEQUENCE_LENGTH, 1), jnp.float32, 0.0, 2.31))
    column_scale = jnp.exp(jax.random.uniform(random_keys[1], (1, 1, D), jnp.float32, 0.0, 2.31))
    values = jax.random.normal(random_keys[2], (SEQUENCE_COUNT, SEQUENCE_LENGTH, D), jnp.float32) * row_scale * column_scale * 0.1
    return jnp.clip(values, -80.0, 80.0).astype(jnp.bfloat16)


def block_scale(own_key, shape, cuts, smallest, high):
    gain = 1.0
    for position, blocks in cuts:
        steps = jax.random.uniform(jax.random.fold_in(jax.random.fold_in(own_key, 6), position), (blocks,), jnp.float32, smallest / len(cuts), high / len(cuts))
        gain = gain * jnp.repeat(jnp.exp(steps), shape[position] // blocks).reshape((-1,) + (1,) * (len(shape) - 1 - position))
    return gain


def gaussian(stream_key, extent, scale, most, cuts=(), dtype=jnp.bfloat16):
    factor_of = block_scale(stream_key, extent, cuts, -0.22, 0.18) if cuts else 1.0
    array = jax.random.normal(stream_key, extent, jnp.float32) * scale * factor_of
    return jnp.minimum(jnp.maximum(array, -most), most).astype(dtype)


def setup_inputs(seed: int = 0) -> dict:
    streams_of = jax.random.split(jax.random.key(seed), 8)
    middle_state = draw_middle_state(jax.random.fold_in(streams_of[7], 71), 0)
    newest_state = gaussian(streams_of[1], (SEQUENCE_COUNT, SEQUENCE_LENGTH, D), 1.0, 6.0, ((0, 16), (1, 8)))
    middle_cotangent = gaussian(streams_of[2], (SEQUENCE_COUNT, SEQUENCE_LENGTH, D), 1.0, 6.0, ((0, 16), (1, 8)))
    newest_cotangent = gaussian(streams_of[3], (SEQUENCE_COUNT, SEQUENCE_LENGTH, D), 1.0, 6.0, ((0, 16), (1, 8)))
    log_decay = draw_log_decay(jax.random.fold_in(streams_of[7], 71), 0)
    state_weights = gaussian(streams_of[5], (D, 2 * N), D ** -0.5, 0.09375, ((0, 16),))
    skip_gain = jnp.clip(jax.random.uniform(streams_of[6], (HALF_HEADS,), jnp.float32, 0.5, 1.5), 0.5, 1.5)
    return dict(middle_state=middle_state, newest_state=newest_state, middle_cotangent=middle_cotangent, newest_cotangent=newest_cotangent, log_decay=log_decay, state_weights=state_weights, skip_gain=skip_gain)


highest = lax.Precision.HIGHEST
norm_epsilon = 1e-05
decay_unit = 1.0 / 4096.0

def normalize(values):
    return values * lax.rsqrt(lax.optimization_barrier(jnp.mean(values * values, axis=-1, keepdims=True)) + norm_epsilon)

def group_pass(state_now, pieces, skip_gain):
    features, entry_key, readout, log_rates = pieces
    length = log_rates.shape[0]
    running = jnp.cumsum(log_rates, axis=0)
    input_feed = jnp.sqrt(1.0 - jnp.exp(2.0 * log_rates))
    inputs = features * input_feed[:, :, None]
    scores = jnp.dot(readout, entry_key.T, precision=highest)
    later_index = lax.broadcasted_iota(jnp.int32, (length, length), 0)
    earlier_index = lax.broadcasted_iota(jnp.int32, (length, length), 1)
    causal = (later_index >= earlier_index)[None]
    heads_first = running.T
    log_gaps = heads_first[:, :, None] - heads_first[:, None, :]
    mix_weights = jnp.where(causal, jnp.exp(jnp.where(causal, log_gaps, 0.0)), 0.0) * scores[None]
    within = jnp.einsum('hts,shp->thp', mix_weights, inputs, precision=highest)
    carried = jnp.einsum('tn,hpn->thp', readout, state_now, precision=highest) * jnp.exp(running)[:, :, None]
    outputs = (within + carried) * N ** (-0.5) + skip_gain[None, :, None] * features
    tail_decay = jnp.exp(running[-1][None, :] - running)
    new_state = state_now * jnp.exp(running[-1])[:, None, None] + jnp.einsum('shp,sn->hpn', inputs * tail_decay[:, :, None], entry_key, precision=highest)
    return (new_state, outputs)

def run_rows(feature_values, projected_values, log_rates, skip_gain, start_state):
    row_count = feature_values.shape[0]
    block_count = row_count // GROUP
    features = feature_values.reshape(block_count, GROUP, HALF_HEADS, P_SIZE)
    entry_key = projected_values[:, :N].reshape(block_count, GROUP, N)
    readout = projected_values[:, N:].reshape(block_count, GROUP, N)
    log_blocks = log_rates.reshape(block_count, GROUP, HALF_HEADS)

    def step_block(state_now, pieces):
        return group_pass(state_now, pieces, skip_gain)
    final_state, outputs = lax.scan(step_block, start_state, (features, entry_key, readout, log_blocks))
    return (outputs.reshape(row_count, HALF_HEADS * P_SIZE), final_state)

def reference(middle_state, newest_state, middle_cotangent, newest_cotangent, log_decay, state_weights, skip_gain):
    row_count = middle_state.shape[1]
    zero_start = jnp.zeros((HALF_HEADS, P_SIZE, N), jnp.float32)

    def per_sequence(running_sum, pieces):
        middle, newest, middle_back, newest_back, log_ints = pieces
        normed, norm_back = jax.vjp(normalize, middle.astype(jnp.float32))
        features = normed.astype(jnp.bfloat16)
        projected = jnp.dot(features, state_weights, preferred_element_type=jnp.float32).astype(jnp.bfloat16)
        log_rates = log_ints.astype(jnp.float32) * decay_unit

        def whole_mix(feature_values, projected_values):
            return run_rows(feature_values, projected_values, log_rates, skip_gain, zero_start)[0]
        mixed_out, mix_back = jax.vjp(whole_mix, features.astype(jnp.float32), projected.astype(jnp.float32))
        rebuilt = (newest.astype(jnp.float32) - mixed_out).astype(jnp.bfloat16)
        feature_grad, projected_grad = mix_back(newest_back.astype(jnp.float32))
        projected_low = projected_grad.astype(jnp.bfloat16)
        through_weights = lax.dot_general(projected_low, state_weights, (((1,), (1,)), ((), ())), preferred_element_type=jnp.float32)
        norm_grad, = norm_back(feature_grad + through_weights)
        gradient = (middle_back.astype(jnp.float32) + norm_grad).astype(jnp.bfloat16)
        weight_term = lax.dot_general(features, projected_low, (((0,), (0,)), ((), ())), preferred_element_type=jnp.float32)
        return (running_sum + weight_term, (rebuilt, gradient))
    total_grad, (rebuilt_all, gradient_all) = lax.scan(per_sequence, jnp.zeros((D, 2 * N), jnp.float32), (middle_state, newest_state, middle_cotangent, newest_cotangent, log_decay))
    return (rebuilt_all, gradient_all, total_grad * (SEQUENCE_COUNT * row_count) ** (-0.5))
```

```python
import jax
import jax.numpy as jnp
from jax import lax
from jax.experimental import pallas as pl
from jax.experimental.pallas import tpu as pltpu
from jax.sharding import PartitionSpec as P

MESH = pl.DeviceIdType.MESH
F32 = jnp.float32
BF = jnp.bfloat16
T = 512
D = 4096
H = 32
N = 128
Q = 512
EPS = 1e-05
UNIT = 1.0 / 4096.0
RN = N ** (-0.5)
SEQ = 8
FS = 16


def dot(a, b):
    return jnp.dot(a, b, preferred_element_type=F32)


def dot_nt(a, b):
    return lax.dot_general(a, b, (((1,), (1,)), ((), ())), preferred_element_type=F32)


def dot_tn(a, b):
    return lax.dot_general(a, b, (((0,), (0,)), ((), ())), preferred_element_type=F32)


def split(v, parts):
    out = []
    for _ in range(parts):
        p = v.astype(BF)
        out.append(p)
        v = v - p.astype(F32)
    return jnp.concatenate(out, axis=1)


def pick(parts, head, heads):
    rows = lax.broadcasted_iota(jnp.int32, (parts * H, heads * N), 0)
    cols = lax.broadcasted_iota(jnp.int32, (parts * H, heads * N), 1)
    return (rows % H == head + cols // N).astype(F32).astype(BF)


def decays(ld):
    v = ld.astype(F32)
    hi = jnp.floor(v * (1.0 / 64.0))
    lo = v - hi * 64.0
    low = lax.broadcasted_iota(jnp.int32, (T, T), 0) >= lax.broadcasted_iota(
        jnp.int32, (T, T), 1
    )
    low = low.astype(F32).astype(BF)
    run = (64.0 * dot(low, hi.astype(BF)) + dot(low, lo.astype(BF))) * UNIT
    feed = jnp.sqrt(1.0 - jnp.exp(2.0 * (v * UNIT)))
    return run, feed


def kernel_a(
    x_ref, g_ref, ld_ref, w_ref,
    X_o, W_o, proj_o, AT_o, GT_o, dec_o, runs_o, lead_o, tail_o, feed_o, runT_o,
    wbuf, ss, rs, cs, cr,
):
    s = lax.axis_index("seq")
    f = lax.axis_index("fsdp")
    sib = f + 1 - 2 * (f % 2)
    barrier = pltpu.get_barrier_semaphore()
    for k in range(1, 8):
        pl.semaphore_signal(
            barrier, inc=1, device_id=(s, (f + 2 * k) % FS), device_id_type=MESH
        )
    pl.semaphore_signal(barrier, inc=1, device_id=(s, sib), device_id_type=MESH)
    pl.semaphore_wait(barrier, 8)

    def slot(i):
        return wbuf.at[pl.ds(pl.multiple_of(i * 256, 256), 256)]

    sends = []
    for k in range(1, 8):
        c = pltpu.make_async_remote_copy(
            w_ref, slot(f), ss.at[k - 1], rs.at[k - 1],
            device_id=(s, (f + 2 * k) % FS), device_id_type=MESH,
        )
        c.start()
        sends.append(c)
    own = pltpu.make_async_remote_copy(
        w_ref, slot(f), cs.at[0], cr.at[0], device_id=(s, sib), device_id_type=MESH
    )
    own.start()
    wbuf[pl.ds(pl.multiple_of(f * 256, 256), 256), :] = w_ref[...]

    def norm(i, _):
        rows = pl.ds(pl.multiple_of(i * 32, 32), 32)
        v = x_ref[rows, :].astype(F32)
        r = lax.rsqrt(jnp.mean(v * v, axis=1, keepdims=True) + EPS)
        X_o[rows, :] = (v * r).astype(BF)
        return 0

    lax.fori_loop(0, T // 32, norm, 0)

    run, feed = decays(ld_ref[...])
    end = run[T - 1 : T, :]
    runs_o[...] = split(run, 3)
    lead_o[...] = split(jnp.exp(run), 2)
    tail_o[...] = split(feed * jnp.exp(end - run), 2)
    feed_o[...] = split(feed, 2)
    wide = jnp.concatenate([run, jnp.zeros((T, N - H), F32)], axis=1)
    runT_o[...] = wide.T[:H, :]
    total = split(jnp.broadcast_to(jnp.exp(end), (8, H)), 3)
    for i in range(8):
        dec_o[:, i * Q : (i + 1) * Q] = dot(total, pick(3, 4 * i, 4))

    passed = []
    for k in range(1, 8):
        sends[k - 1].wait_recv()
        at = (f + FS - 2 * k) % FS
        c = pltpu.make_async_remote_copy(
            slot(at), slot(at), cs.at[k], cr.at[k],
            device_id=(s, sib), device_id_type=MESH,
        )
        c.start()
        passed.append(c)
    own.wait()
    for c in passed:
        c.wait()
    for c in sends:
        c.wait_send()

    def project(i, _):
        rows = pl.ds(pl.multiple_of(i * 128, 128), 128)
        proj_o[rows, :] = dot(X_o[rows, :], wbuf[...]).astype(BF)
        return 0

    lax.fori_loop(0, 4, project, 0)
    W_o[...] = wbuf[...]
    BT = proj_o[:, :N].astype(F32).T.astype(BF)
    CT = proj_o[:, N:].astype(F32).T.astype(BF)

    def states(i, _):
        cols = pl.ds(pl.multiple_of(i * Q, Q), Q)
        sel = pick(2, 4 * i, 4)
        xs = (X_o[:, cols].astype(F32) * dot(tail_o[...], sel)).astype(BF)
        AT_o[:, cols] = dot(BT, xs).astype(BF)
        gs = (g_ref[:, cols].astype(F32) * dot(lead_o[...], sel)).astype(BF)
        GT_o[:, cols] = (dot(CT, gs) * RN).astype(BF)
        return 0

    lax.fori_loop(0, 8, states, 0)


def kernel_b(
    gain_ref, X_ref, g_ref, proj_ref, AT_ref, GT_ref, dec_ref, runs_ref, feed_ref, runT_ref,
    S_o, G_o, mix_o, dx_o, dS_o,
    sc, a_in, g_in, d_in, a_out, g_out, S_buf, G_buf,
    s1, r1, s2, r2, s3, r3, s4, r4, s5, r5,
):
    s = lax.axis_index("seq")
    f = lax.axis_index("fsdp")
    barrier = pltpu.get_barrier_semaphore()
    for k in range(1, SEQ):
        pl.semaphore_signal(
            barrier, inc=1, device_id=((s + k) % SEQ, f), device_id_type=MESH
        )
    pl.semaphore_wait(barrier, SEQ - 1)

    def part(ref, i):
        return ref.at[:, pl.ds(pl.multiple_of(i * Q, Q), Q)]

    def send(src, dst, a, b, k):
        c = pltpu.make_async_remote_copy(
            src, dst, a.at[k - 1], b.at[k - 1],
            device_id=((s + k) % SEQ, f), device_id_type=MESH,
        )
        c.start()
        return c

    mine = pl.ds(pl.multiple_of(s * Q, Q), Q)
    decs, first, second = [], [], []
    for k in range(1, SEQ):
        to = (s + k) % SEQ
        decs.append(send(part(dec_ref, to), d_in.at[s], s5, r5, k))
        first.append(send(part(AT_ref, to), a_in.at[s], s1, r1, k))
    for k in range(1, SEQ):
        to = (s + k) % SEQ
        second.append(send(part(GT_ref, to), g_in.at[s], s2, r2, k))
    a_in[pl.ds(s, 1)] = AT_ref[:, mine][None]
    g_in[pl.ds(s, 1)] = GT_ref[:, mine][None]
    d_in[pl.ds(s, 1)] = dec_ref[:, mine][None]

    B = proj_ref[:, :N]
    C = proj_ref[:, N:]
    sc[...] = dot_nt(C, B) * RN
    dS_o[...] = jnp.zeros_like(dS_o)
    tri = lax.broadcasted_iota(jnp.int32, (N, N), 0) >= lax.broadcasted_iota(
        jnp.int32, (N, N), 1
    )

    def head(h, _):
        cols = pl.ds(pl.multiple_of(h * N, N), N)
        gain = gain_ref[h]
        run_b = dot(runs_ref[...], pick(3, h, 1))
        feed_b = dot(feed_ref[...], pick(2, h, 1))
        x = X_ref[:, cols].astype(F32)
        xf = (x * feed_b).astype(BF)
        g = g_ref[:, cols]
        row = runT_ref[pl.ds(h, 1), :]
        w = [[None] * 4 for _ in range(4)]
        for i in range(4):
            ri = slice(i * N, (i + 1) * N)
            dP = dot_nt(g[ri], xf[: (i + 1) * N])
            for j in range(i + 1):
                rj = slice(j * N, (j + 1) * N)
                d = run_b[ri] - row[:, rj]
                if i == j:
                    e = jnp.where(tri, jnp.exp(jnp.minimum(d, 0.0)), 0.0)
                else:
                    e = jnp.exp(d)
                dS_o[ri, rj] += e * dP[:, rj]
                w[i][j] = (e * sc[ri, rj]).astype(BF)
            wi = w[i][0] if i == 0 else jnp.concatenate(w[i][: i + 1], axis=1)
            m = dot(wi, xf[: (i + 1) * N]) + gain * x[ri]
            mix_o[ri, cols] = m.astype(BF)
        for j in range(4):
            rj = slice(j * N, (j + 1) * N)
            wj = [w[i][j] for i in range(j, 4)]
            wj = wj[0] if len(wj) == 1 else jnp.concatenate(wj, axis=0)
            dx = dot_tn(wj, g[j * N :]) * feed_b[rj] + gain * g[rj].astype(F32)
            dx_o[rj, cols] = dx.astype(BF)
        return 0

    lax.fori_loop(0, H // 2, head, 0)

    for c in decs + first:
        c.wait()
    state = jnp.zeros((N, Q), F32)
    for j in range(SEQ):
        a_out[j] = state.astype(BF)
        if j < SEQ - 1:
            state = d_in[j, 0:1, :] * state + a_in[j].astype(F32)
    third = []
    for k in range(1, SEQ):
        to = (s + k) % SEQ
        third.append(send(a_out.at[to], part(S_buf, s), s3, r3, k))
    S_buf[:, mine] = a_out[pl.ds(s, 1)][0]

    lax.fori_loop(H // 2, H, head, 0)

    for c in second:
        c.wait()
    state = jnp.zeros((N, Q), F32)
    for j in range(SEQ - 1, -1, -1):
        g_out[j] = state.astype(BF)
        if j > 0:
            state = d_in[j, 0:1, :] * state + g_in[j].astype(F32)
    fourth = []
    for k in range(1, SEQ):
        to = (s + k) % SEQ
        fourth.append(send(g_out.at[to], part(G_buf, s), s4, r4, k))
    G_buf[:, mine] = g_out[pl.ds(s, 1)][0]
    for c in third:
        c.wait()
    S_o[...] = S_buf[...]
    for c in fourth:
        c.wait()
    G_o[...] = G_buf[...]


def kernel_c(
    X_ref, g_ref, mix_ref, dx_ref, new_ref, S_ref, G_ref, proj_ref, lead_ref, tail_ref, dS_ref,
    old_o, fg_o, pl_o, dB, dC,
):
    i = pl.program_id(0)

    @pl.when(i == 0)
    def _():
        dB[...] = jnp.zeros_like(dB)
        dC[...] = jnp.zeros_like(dC)

    B = proj_ref[:, :N]
    C = proj_ref[:, N:]
    sel = pick(2, 4 * i, 4)
    lead = dot(lead_ref[...], sel) * RN
    tail = dot(tail_ref[...], sel)
    S = S_ref[...]
    G = G_ref[...]
    mixed = dot(C, S) * lead + mix_ref[...].astype(F32)
    old_o[...] = (new_ref[...].astype(F32) - mixed).astype(BF)
    fg_o[...] = (dot(B, G) * tail + dx_ref[...].astype(F32)).astype(BF)
    gs = (g_ref[...].astype(F32) * lead).astype(BF)
    dC[...] += dot_nt(gs, S)
    xs = (X_ref[...].astype(F32) * tail).astype(BF)
    dB[...] += dot_nt(xs, G)

    @pl.when(i == pl.num_programs(0) - 1)
    def _():
        dS = (dS_ref[...] * RN).astype(BF)
        pl_o[:, N:] = (dC[...] + dot(dS, B)).astype(BF)
        pl_o[:, :N] = (dB[...] + dot_tn(dS, C)).astype(BF)


def kernel_d(
    X_ref, pl_ref, o_ref, part, r1buf, acc1, r2buf, acc2, r3buf, s1, r1, s2, r2, s3, r3
):
    s = lax.axis_index("seq")
    f = lax.axis_index("fsdp")
    core = f % 2
    chip = f // 2
    sib = f + 1 - 2 * core
    barrier = pltpu.get_barrier_semaphore()
    for k in range(1, 8):
        pl.semaphore_signal(
            barrier, inc=1, device_id=(s, (f + 2 * k) % FS), device_id_type=MESH
        )
        pl.semaphore_signal(
            barrier, inc=1, device_id=((s + k) % SEQ, f), device_id_type=MESH
        )
    pl.semaphore_signal(barrier, inc=1, device_id=(s, sib), device_id_type=MESH)
    pl.semaphore_wait(barrier, 15)

    low = pl_ref[...]

    def product(i, _):
        cols = pl.ds(pl.multiple_of(i * Q, Q), Q)
        v = dot_tn(X_ref[:, cols], low).astype(BF)
        part[pl.ds(i, 1)] = v.reshape(1, 8, 2, 32, 256)
        return 0

    lax.fori_loop(0, 8, product, 0)
    c = pltpu.make_async_remote_copy(
        part.at[:, :, 1 - core], r1buf, s1, r1,
        device_id=(s, sib), device_id_type=MESH,
    )
    c.start()
    c.wait()
    own = part[:, :, pl.ds(core, 1)].reshape(8, 8, 32, 256)
    acc1[...] = (own.astype(F32) + r1buf[...].astype(F32)).astype(BF)
    cs = []
    for k in range(1, 8):
        to = (chip + k) % 8
        c = pltpu.make_async_remote_copy(
            acc1.at[:, to], r2buf.at[k - 1], s2.at[k - 1], r2.at[k - 1],
            device_id=(s, (f + 2 * k) % FS), device_id_type=MESH,
        )
        c.start()
        cs.append(c)
    total = acc1[:, pl.ds(chip, 1)].reshape(8, 32, 256).astype(F32)
    for k in range(7):
        cs[k].wait()
        total += r2buf[k].astype(F32)
    acc2[...] = total.astype(BF)
    cs = []
    for k in range(1, 8):
        to = (s + k) % SEQ
        c = pltpu.make_async_remote_copy(
            acc2.at[to], r3buf.at[k - 1], s3.at[k - 1], r3.at[k - 1],
            device_id=(to, f), device_id_type=MESH,
        )
        c.start()
        cs.append(c)
    total = acc2[pl.ds(s, 1)].reshape(32, 256).astype(F32)
    for k in range(7):
        cs[k].wait()
        total += r3buf[k].astype(F32)
    o_ref[...] = total * (T * SEQ * FS) ** (-0.5)


def kernel_e(x_ref, fg_ref, pl_ref, cot_ref, W_ref, o_ref, ng):
    low = pl_ref[...]
    rows = low.shape[0]
    xx = jnp.zeros((rows, 1), F32)
    xg = jnp.zeros((rows, 1), F32)
    for i in range(8):
        cols = slice(i * Q, (i + 1) * Q)
        x = x_ref[:, cols].astype(F32)
        v = dot_nt(low, W_ref[cols, :]) + fg_ref[:, cols].astype(F32)
        ng[:, cols] = v
        xx += jnp.sum(x * x, axis=1, keepdims=True)
        xg += jnp.sum(x * v, axis=1, keepdims=True)
    r = lax.rsqrt(xx * (1.0 / D) + EPS)
    back = r * r * r * xg * (1.0 / D)
    for i in range(8):
        cols = slice(i * Q, (i + 1) * Q)
        x = x_ref[:, cols].astype(F32)
        o_ref[:, cols] = (
            cot_ref[:, cols].astype(F32) + (r * ng[:, cols] - back * x)
        ).astype(BF)


def shape(*dims, dtype=BF):
    return jax.ShapeDtypeStruct(dims, dtype)


VM = pl.BlockSpec(memory_space=pltpu.VMEM)
DMA = pltpu.SemaphoreType.DMA
LIMIT = 56 << 20


def shards(middle, newest, middle_cot, newest_cot, log_decay, weights, gain):
    x, new, cot, g, ld = middle[0], newest[0], middle_cot[0], newest_cot[0], log_decay[0]

    def remote(cid):
        return pltpu.CompilerParams(
            collective_id=cid, has_side_effects=True, vmem_limit_bytes=LIMIT
        )

    X, W, proj, AT, GT, dec, runs, lead, tail, feed, runT = pl.pallas_call(
        kernel_a,
        name="gather",
        out_shape=[
            shape(T, D), shape(D, 2 * N), shape(T, 2 * N), shape(N, D), shape(N, D),
            shape(8, D, dtype=F32), shape(T, 3 * H), shape(T, 2 * H), shape(T, 2 * H), shape(T, 2 * H),
            shape(H, T, dtype=F32),
        ],
        in_specs=[VM] * 4,
        out_specs=[VM] * 11,
        scratch_shapes=[
            pltpu.VMEM((D, 2 * N), BF), DMA((7,)), DMA((7,)), DMA((8,)), DMA((8,)),
        ],
        compiler_params=remote(0),
    )(x, g, ld, weights)

    S, G, mix, dx, dS = pl.pallas_call(
        kernel_b,
        name="exchange",
        out_shape=[shape(N, D), shape(N, D), shape(T, D), shape(T, D), shape(T, T, dtype=F32)],
        in_specs=[pl.BlockSpec(memory_space=pltpu.SMEM)] + [VM] * 9,
        out_specs=[VM] * 5,
        scratch_shapes=[
            pltpu.VMEM((T, T), F32),
            pltpu.VMEM((SEQ, N, Q), BF), pltpu.VMEM((SEQ, N, Q), BF), pltpu.VMEM((SEQ, 8, Q), F32),
            pltpu.VMEM((SEQ, N, Q), BF), pltpu.VMEM((SEQ, N, Q), BF),
            pltpu.VMEM((N, D), BF), pltpu.VMEM((N, D), BF),
        ] + [DMA((7,))] * 10,
        compiler_params=remote(1),
    )(gain, X, g, proj, AT, GT, dec, runs, feed, runT)

    def cols(rows):
        return pl.BlockSpec((rows, Q), lambda i: (0, i))

    def whole(a):
        return pl.BlockSpec(a.shape, lambda i: (0, 0))

    old, fg, low = pl.pallas_call(
        kernel_c,
        name="carried",
        grid=(8,),
        out_shape=[shape(T, D), shape(T, D), shape(T, 2 * N)],
        in_specs=[cols(T)] * 5 + [cols(N)] * 2 + [whole(proj), whole(lead), whole(tail), whole(dS)],
        out_specs=[cols(T), cols(T), pl.BlockSpec((T, 2 * N), lambda i: (0, 0))],
        scratch_shapes=[pltpu.VMEM((T, N), F32), pltpu.VMEM((T, N), F32)],
        compiler_params=pltpu.CompilerParams(vmem_limit_bytes=LIMIT),
    )(X, g, mix, dx, new, S, G, proj, lead, tail, dS)

    grad = pl.pallas_call(
        kernel_d,
        name="reduce",
        out_shape=shape(32, 2 * N, dtype=F32),
        in_specs=[VM] * 2,
        out_specs=VM,
        scratch_shapes=[
            pltpu.VMEM((8, 8, 2, 32, 256), BF), pltpu.VMEM((8, 8, 32, 256), BF),
            pltpu.VMEM((8, 8, 32, 256), BF), pltpu.VMEM((7, 8, 32, 256), BF),
            pltpu.VMEM((8, 32, 256), BF), pltpu.VMEM((7, 32, 256), BF),
            DMA, DMA, DMA((7,)), DMA((7,)), DMA((7,)), DMA((7,)),
        ],
        compiler_params=remote(2),
    )(X, low)

    R = 128
    rows = pl.BlockSpec((R, D), lambda i: (i, 0))
    out = pl.pallas_call(
        kernel_e,
        name="normback",
        grid=(T // R,),
        out_shape=shape(T, D),
        in_specs=[rows, rows, pl.BlockSpec((R, 2 * N), lambda i: (i, 0)), rows, whole(W)],
        out_specs=rows,
        scratch_shapes=[pltpu.VMEM((R, D), F32)],
        compiler_params=pltpu.CompilerParams(vmem_limit_bytes=LIMIT),
    )(x, fg, low, cot, W)
    return old[None], out[None], grad


def solution(mesh):
    return jax.shard_map(
        shards,
        mesh=mesh,
        in_specs=(P("fsdp", "seq", None),) * 5 + (P("fsdp", None), P()),
        out_specs=(P("fsdp", "seq", None), P("fsdp", "seq", None), P(("seq", "fsdp"), None)),
        check_vma=False,
    )
```

```python
import jax
import jax.numpy as jnp
from jax import lax
from jax.experimental import pallas as pl
from jax.experimental.pallas import tpu as pltpu
from jax.sharding import PartitionSpec as P

MESH = pl.DeviceIdType.MESH
F32 = jnp.float32
BF = jnp.bfloat16
T = 512
D = 4096
H = 32
N = 128
Q = 512
EPS = 1e-05
UNIT = 1.0 / 4096.0
RN = N ** (-0.5)
SEQ = 8
FS = 16


def dot(a, b):
    return jnp.dot(a, b, preferred_element_type=F32)


def dot_nt(a, b):
    return lax.dot_general(a, b, (((1,), (1,)), ((), ())), preferred_element_type=F32)


def dot_tn(a, b):
    return lax.dot_general(a, b, (((0,), (0,)), ((), ())), preferred_element_type=F32)


def split(v, parts):
    out = []
    for _ in range(parts):
        p = v.astype(BF)
        out.append(p)
        v = v - p.astype(F32)
    return jnp.concatenate(out, axis=1)


def pick(parts, head, heads):
    rows = lax.broadcasted_iota(jnp.int32, (parts * H, heads * N), 0)
    cols = lax.broadcasted_iota(jnp.int32, (parts * H, heads * N), 1)
    return (rows % H == head + cols // N).astype(F32).astype(BF)


def decays(ld):
    v = ld.astype(F32)
    hi = jnp.floor(v * (1.0 / 64.0))
    lo = v - hi * 64.0
    low = lax.broadcasted_iota(jnp.int32, (T, T), 0) >= lax.broadcasted_iota(
        jnp.int32, (T, T), 1
    )
    low = low.astype(F32).astype(BF)
    run = (64.0 * dot(low, hi.astype(BF)) + dot(low, lo.astype(BF))) * UNIT
    feed = jnp.sqrt(1.0 - jnp.exp(2.0 * (v * UNIT)))
    return run, feed


def whole_step(
    gain_ref, x_hbm, new_hbm, cot_hbm, g_hbm, ld_ref, w_ref,
    old_hbm, grad_hbm, dw_ref,
    xb, X, gb, nb, cb, W, r_ref, proj, AT, GT, dec, runs, lead_s, tail_s, feed_s, runT,
    sc, dS, mix, dx, a_in, g_in, d_in, a_out, g_out, S_buf, G_buf, dB, dC, low, ng,
    part, r1buf, acc1, r2buf, acc2, r3buf,
    lsem, osem, gsem, ss, rs, cs, cr, s1, r1, s2, r2, s3, r3, s4, r4, s5, r5,
    u1, v1, u2, v2, u3, v3,
):
    s = lax.axis_index("seq")
    f = lax.axis_index("fsdp")
    core = f % 2
    chip = f // 2
    sib = f + 1 - 2 * core

    loads = []
    for k, (a, b) in enumerate(((x_hbm, xb), (g_hbm, gb), (new_hbm, nb), (cot_hbm, cb))):
        c = pltpu.make_async_copy(a, b, lsem.at[k])
        c.start()
        loads.append(c)

    barrier = pltpu.get_barrier_semaphore()
    for k in range(1, 8):
        pl.semaphore_signal(
            barrier, inc=1, device_id=(s, (f + 2 * k) % FS), device_id_type=MESH
        )
        pl.semaphore_signal(
            barrier, inc=1, device_id=((s + k) % SEQ, f), device_id_type=MESH
        )
    pl.semaphore_signal(barrier, inc=1, device_id=(s, sib), device_id_type=MESH)
    pl.semaphore_wait(barrier, 15)

    def slot(i):
        return W.at[pl.ds(pl.multiple_of(i * 256, 256), 256)]

    sends = []
    for k in range(1, 8):
        c = pltpu.make_async_remote_copy(
            w_ref, slot(f), ss.at[k - 1], rs.at[k - 1],
            device_id=(s, (f + 2 * k) % FS), device_id_type=MESH,
        )
        c.start()
        sends.append(c)
    own = pltpu.make_async_remote_copy(
        w_ref, slot(f), cs.at[0], cr.at[0], device_id=(s, sib), device_id_type=MESH
    )
    own.start()
    W[pl.ds(pl.multiple_of(f * 256, 256), 256), :] = w_ref[...]

    run, feed = decays(ld_ref[...])
    end = run[T - 1 : T, :]
    runs[...] = split(run, 3)
    lead_s[...] = split(jnp.exp(run), 2)
    tail_s[...] = split(feed * jnp.exp(end - run), 2)
    feed_s[...] = split(feed, 2)
    wide = jnp.concatenate([run, jnp.zeros((T, N - H), F32)], axis=1)
    runT[...] = wide.T[:H, :]
    total = split(jnp.broadcast_to(jnp.exp(end), (8, H)), 3)
    for i in range(8):
        dec[i] = dot(total, pick(3, 4 * i, 4))

    loads[0].wait()

    def norm(i, _):
        rows = pl.ds(pl.multiple_of(i * 32, 32), 32)
        v = xb[rows, :].astype(F32)
        r = lax.rsqrt(jnp.mean(v * v, axis=1, keepdims=True) + EPS)
        r_ref[rows, :] = r
        X[rows, :] = (v * r).astype(BF)
        return 0

    lax.fori_loop(0, T // 32, norm, 0)

    passed = []
    for k in range(1, 8):
        sends[k - 1].wait_recv()
        at = (f + FS - 2 * k) % FS
        c = pltpu.make_async_remote_copy(
            slot(at), slot(at), cs.at[k], cr.at[k],
            device_id=(s, sib), device_id_type=MESH,
        )
        c.start()
        passed.append(c)
    loads[1].wait()
    own.wait()
    for c in passed:
        c.wait()

    def project(i, _):
        rows = pl.ds(pl.multiple_of(i * 128, 128), 128)
        proj[rows, :] = dot(X[rows, :], W[...]).astype(BF)
        return 0

    lax.fori_loop(0, 4, project, 0)
    B = proj[:, :N]
    C = proj[:, N:]
    BT = B.astype(F32).T.astype(BF)
    CT = C.astype(F32).T.astype(BF)

    def peer(src, dst, a, b, k):
        return pltpu.make_async_remote_copy(
            src, dst, a.at[k], b.at[k],
            device_id=((s + k) % SEQ, f), device_id_type=MESH,
        )

    def to_dec(k):
        return peer(dec.at[(s + k) % SEQ], d_in.at[s], s5, r5, k)

    def to_a(k):
        return peer(AT.at[(s + k) % SEQ], a_in.at[s], s1, r1, k)

    def to_g(k):
        return peer(GT.at[(s + k) % SEQ], g_in.at[s], s2, r2, k)

    def back_a(k):
        return peer(a_out.at[(s + k) % SEQ], S_buf.at[s], s3, r3, k)

    def back_g(k):
        return peer(g_out.at[(s + k) % SEQ], G_buf.at[s], s4, r4, k)

    def make_a(k, _):
        i = (s + k) % SEQ
        cols = pl.ds(pl.multiple_of(i * Q, Q), Q)
        sel = pick(2, 4 * i, 4)
        xs = (X[:, cols].astype(F32) * dot(tail_s[...], sel)).astype(BF)
        AT[i] = dot(BT, xs).astype(BF)

        @pl.when(k < SEQ)
        def _():
            to_dec(k).start()
            to_a(k).start()

        return 0

    def make_g(k, _):
        i = (s + k) % SEQ
        cols = pl.ds(pl.multiple_of(i * Q, Q), Q)
        sel = pick(2, 4 * i, 4)
        gs = (gb[:, cols].astype(F32) * dot(lead_s[...], sel)).astype(BF)
        GT[i] = (dot(CT, gs) * RN).astype(BF)

        @pl.when(k < SEQ)
        def _():
            to_g(k).start()

        return 0

    lax.fori_loop(1, SEQ + 1, make_a, 0)
    lax.fori_loop(1, SEQ + 1, make_g, 0)
    a_in[pl.ds(s, 1)] = AT[pl.ds(s, 1)]
    g_in[pl.ds(s, 1)] = GT[pl.ds(s, 1)]
    d_in[pl.ds(s, 1)] = dec[pl.ds(s, 1)]

    sc[...] = dot_nt(C, B) * RN
    dS[...] = jnp.zeros_like(dS)
    dB[...] = jnp.zeros_like(dB)
    dC[...] = jnp.zeros_like(dC)
    tri = lax.broadcasted_iota(jnp.int32, (N, N), 0) >= lax.broadcasted_iota(
        jnp.int32, (N, N), 1
    )

    def head(h, _):
        cols = pl.ds(pl.multiple_of(h * N, N), N)
        gain = gain_ref[h]
        run_b = dot(runs[...], pick(3, h, 1))
        feed_b = dot(feed_s[...], pick(2, h, 1))
        x = X[:, cols].astype(F32)
        xf = (x * feed_b).astype(BF)
        g = gb[:, cols]
        row = runT[pl.ds(h, 1), :]
        w = [[None] * 4 for _ in range(4)]
        for i in range(4):
            ri = slice(i * N, (i + 1) * N)
            dP = dot_nt(g[ri], xf[: (i + 1) * N])
            for j in range(i + 1):
                rj = slice(j * N, (j + 1) * N)
                d = run_b[ri] - row[:, rj]
                if i == j:
                    e = jnp.where(tri, jnp.exp(jnp.minimum(d, 0.0)), 0.0)
                else:
                    e = jnp.exp(d)
                dS[ri, rj] += e * dP[:, rj]
                w[i][j] = (e * sc[ri, rj]).astype(BF)
            wi = w[i][0] if i == 0 else jnp.concatenate(w[i][: i + 1], axis=1)
            m = dot(wi, xf[: (i + 1) * N]) + gain * x[ri]
            mix[ri, cols] = m.astype(BF)
        for j in range(4):
            rj = slice(j * N, (j + 1) * N)
            wj = [w[i][j] for i in range(j, 4)]
            wj = wj[0] if len(wj) == 1 else jnp.concatenate(wj, axis=0)
            v = dot_tn(wj, g[j * N :]) * feed_b[rj] + gain * g[rj].astype(F32)
            dx[rj, cols] = v.astype(BF)
        return 0

    def wait_in(make):
        def one(k, _):
            make(k).wait()
            return 0

        lax.fori_loop(1, SEQ, one, 0)

    def start_back(make):
        def one(k, _):
            make(k).start()
            return 0

        lax.fori_loop(1, SEQ, one, 0)

    lax.fori_loop(0, HEADS_1, head, 0)

    wait_in(to_dec)
    wait_in(to_a)
    state = jnp.zeros((N, Q), F32)
    for j in range(SEQ):
        a_out[j] = state.astype(BF)
        if j < SEQ - 1:
            state = d_in[j, 0:1, :] * state + a_in[j].astype(F32)
    start_back(back_a)
    S_buf[pl.ds(s, 1)] = a_out[pl.ds(s, 1)]

    lax.fori_loop(HEADS_1, HEADS_2, head, 0)

    wait_in(to_g)
    state = jnp.zeros((N, Q), F32)
    for j in range(SEQ - 1, -1, -1):
        g_out[j] = state.astype(BF)
        if j > 0:
            state = d_in[j, 0:1, :] * state + g_in[j].astype(F32)
    start_back(back_g)
    G_buf[pl.ds(s, 1)] = g_out[pl.ds(s, 1)]

    lax.fori_loop(HEADS_2, H, head, 0)
    loads[2].wait()

    def old_copy(i):
        cols = pl.ds(pl.multiple_of(i * Q, Q), Q)
        return pltpu.make_async_copy(nb.at[:, cols], old_hbm.at[:, cols], osem.at[i])

    def carried(k, _):
        @pl.when(k > 0)
        def _():
            back_a(k).wait()

        i = (s + SEQ - k) % SEQ
        cols = pl.ds(pl.multiple_of(i * Q, Q), Q)
        lead = dot(lead_s[...], pick(2, 4 * i, 4)) * RN
        S = S_buf[i]
        mixed = dot(C, S) * lead + mix[:, cols].astype(F32)
        nb[:, cols] = (nb[:, cols].astype(F32) - mixed).astype(BF)
        old_copy(i).start()
        gs = (gb[:, cols].astype(F32) * lead).astype(BF)
        dC[...] += dot_nt(gs, S)
        return 0

    lax.fori_loop(0, SEQ, carried, 0)

    dSl = (dS[...] * RN).astype(BF)
    low[:, N:] = (dC[...] + dot(dSl, B)).astype(BF)
    dB[...] = dot_tn(dSl, C)

    def carried_back(k, _):
        @pl.when(k > 0)
        def _():
            back_g(k).wait()

        i = (s + SEQ - k) % SEQ
        cols = pl.ds(pl.multiple_of(i * Q, Q), Q)
        tail = dot(tail_s[...], pick(2, 4 * i, 4))
        G = G_buf[i]
        xs = (X[:, cols].astype(F32) * tail).astype(BF)
        dB[...] += dot_nt(xs, G)
        dx[:, cols] = (dot(B, G) * tail + dx[:, cols].astype(F32)).astype(BF)
        return 0

    lax.fori_loop(0, SEQ, carried_back, 0)
    low[:, :N] = dB[...].astype(BF)

    def to_sib(i):
        return pltpu.make_async_remote_copy(
            part.at[i, :, 1 - core], r1buf.at[i], u1.at[i], v1.at[i],
            device_id=(s, sib), device_id_type=MESH,
        )

    def product(i, _):
        cols = pl.ds(pl.multiple_of(i * Q, Q), Q)
        v = dot_tn(X[:, cols], low[...]).astype(BF)
        part[pl.ds(i, 1)] = v.reshape(1, 8, 2, 32, 256)
        to_sib(i).start()
        return 0

    lax.fori_loop(0, SEQ, product, 0)

    def join(i, _):
        to_sib(i).wait()
        mine = part[pl.ds(i, 1), :, pl.ds(core, 1)].reshape(8, 32, 256)
        acc1[i] = (mine.astype(F32) + r1buf[i].astype(F32)).astype(BF)
        return 0

    lax.fori_loop(0, SEQ, join, 0)

    def to_chip(k):
        return pltpu.make_async_remote_copy(
            acc1.at[:, (chip + k) % 8], r2buf.at[k - 1], u2.at[k - 1], v2.at[k - 1],
            device_id=(s, (f + 2 * k) % FS), device_id_type=MESH,
        )

    for k in range(1, 8):
        to_chip(k).start()

    loads[3].wait()

    def grad_copy(b):
        rows = pl.ds(pl.multiple_of(b * 128, 128), 128)
        return pltpu.make_async_copy(cb.at[rows], grad_hbm.at[rows], gsem.at[b])

    def normback(b, _):
        rows = pl.ds(pl.multiple_of(b * 128, 128), 128)
        lo = low[rows, :]
        xg = jnp.zeros((128, N), F32)
        for i in range(8):
            cols = slice(i * Q, (i + 1) * Q)
            v = dot_nt(lo, W[cols, :]) + dx[rows, cols].astype(F32)
            ng[:, cols] = v
            t = xb[rows, cols].astype(F32) * v
            xg += t[:, :N] + t[:, N : 2 * N] + t[:, 2 * N : 3 * N] + t[:, 3 * N :]
        r = r_ref[rows, :]
        back = r * r * r * (jnp.sum(xg, axis=1, keepdims=True) * (1.0 / D))
        for i in range(8):
            cols = slice(i * Q, (i + 1) * Q)
            v = r * ng[:, cols] - back * xb[rows, cols].astype(F32)
            cb[rows, cols] = (cb[rows, cols].astype(F32) + v).astype(BF)
        grad_copy(b).start()
        return 0

    lax.fori_loop(0, 4, normback, 0)

    total = acc1[:, pl.ds(chip, 1)].reshape(8, 32, 256).astype(F32)
    for k in range(1, 8):
        to_chip(k).wait()
        total += r2buf[k - 1].astype(F32)
    acc2[...] = total.astype(BF)

    def to_seq(k):
        return pltpu.make_async_remote_copy(
            acc2.at[(s + k) % SEQ], r3buf.at[k - 1], u3.at[k - 1], v3.at[k - 1],
            device_id=((s + k) % SEQ, f), device_id_type=MESH,
        )

    for k in range(1, 8):
        to_seq(k).start()
    for c in sends:
        c.wait_send()
    for i in range(SEQ):
        old_copy(i).wait()
    for b in range(4):
        grad_copy(b).wait()
    total = acc2[pl.ds(s, 1)].reshape(32, 256).astype(F32)
    for k in range(1, 8):
        to_seq(k).wait()
        total += r3buf[k - 1].astype(F32)
    dw_ref[...] = total * (T * SEQ * FS) ** (-0.5)


def shape(*dims, dtype=BF):
    return jax.ShapeDtypeStruct(dims, dtype)


HEADS_1 = 12
HEADS_2 = 24
VM = pl.BlockSpec(memory_space=pltpu.VMEM)
ANY = pl.BlockSpec(memory_space=pl.ANY)
DMA = pltpu.SemaphoreType.DMA
LIMIT = 60 << 20


def shards(middle, newest, middle_cot, newest_cot, log_decay, weights, gain):
    def vm(*dims, dtype=BF):
        return pltpu.VMEM(dims, dtype)

    scratch = [
        vm(T, D), vm(T, D), vm(T, D), vm(T, D), vm(T, D), vm(D, 2 * N), vm(T, 1, dtype=F32),
        vm(T, 2 * N), vm(SEQ, N, Q), vm(SEQ, N, Q), vm(SEQ, 8, Q, dtype=F32),
        vm(T, 3 * H), vm(T, 2 * H), vm(T, 2 * H), vm(T, 2 * H), vm(H, T, dtype=F32),
        vm(T, T, dtype=F32), vm(T, T, dtype=F32), vm(T, D), vm(T, D),
        vm(SEQ, N, Q), vm(SEQ, N, Q), vm(SEQ, 8, Q, dtype=F32),
        vm(SEQ, N, Q), vm(SEQ, N, Q), vm(SEQ, N, Q), vm(SEQ, N, Q),
        vm(T, N, dtype=F32), vm(T, N, dtype=F32), vm(T, 2 * N), vm(128, D, dtype=F32),
        vm(8, 8, 2, 32, 256), vm(8, 8, 32, 256), vm(8, 8, 32, 256), vm(7, 8, 32, 256),
        vm(8, 32, 256), vm(7, 32, 256),
        DMA((4,)), DMA((8,)), DMA((4,)), DMA((7,)), DMA((7,)), DMA((8,)), DMA((8,)),
    ] + [DMA((8,))] * 10 + [DMA((8,)), DMA((8,))] + [DMA((7,))] * 4
    old, out, grad = pl.pallas_call(
        whole_step,
        name="step",
        out_shape=[shape(T, D), shape(T, D), shape(32, 2 * N, dtype=F32)],
        in_specs=[pl.BlockSpec(memory_space=pltpu.SMEM)] + [ANY] * 4 + [VM] * 2,
        out_specs=[ANY, ANY, VM],
        scratch_shapes=scratch,
        compiler_params=pltpu.CompilerParams(
            collective_id=0, has_side_effects=True, vmem_limit_bytes=LIMIT
        ),
    )(gain, middle[0], newest[0], middle_cot[0], newest_cot[0], log_decay[0], weights)
    return old[None], out[None], grad


def solution(mesh):
    return jax.shard_map(
        shards,
        mesh=mesh,
        in_specs=(P("fsdp", "seq", None),) * 5 + (P("fsdp", None), P()),
        out_specs=(P("fsdp", "seq", None), P("fsdp", "seq", None), P(("seq", "fsdp"), None)),
        check_vma=False,
    )
```

```python
import jax
import jax.numpy as jnp
from jax import lax
from jax.experimental import pallas as pl
from jax.experimental.pallas import tpu as pltpu
from jax.sharding import PartitionSpec as P

MESH = pl.DeviceIdType.MESH
F32 = jnp.float32
BF = jnp.bfloat16
T = 512
D = 4096
H = 32
N = 128
Q = 512
EPS = 1e-05
UNIT = 1.0 / 4096.0
RN = N ** (-0.5)
SEQ = 8
FS = 16


def dot(a, b):
    return jnp.dot(a, b, preferred_element_type=F32)


def dot_nt(a, b):
    return lax.dot_general(a, b, (((1,), (1,)), ((), ())), preferred_element_type=F32)


def dot_tn(a, b):
    return lax.dot_general(a, b, (((0,), (0,)), ((), ())), preferred_element_type=F32)


def split(v, parts):
    out = []
    for _ in range(parts):
        p = v.astype(BF)
        out.append(p)
        v = v - p.astype(F32)
    return jnp.concatenate(out, axis=1)


def pick(parts, head, heads):
    rows = lax.broadcasted_iota(jnp.int32, (parts * H, heads * N), 0)
    cols = lax.broadcasted_iota(jnp.int32, (parts * H, heads * N), 1)
    return (rows % H == head + cols // N).astype(F32).astype(BF)


def decays(ld):
    v = ld.astype(F32)
    hi = jnp.floor(v * (1.0 / 64.0))
    lo = v - hi * 64.0
    up = lax.broadcasted_iota(jnp.int32, (T, T), 0) <= lax.broadcasted_iota(
        jnp.int32, (T, T), 1
    )
    up = up.astype(F32).astype(BF)
    run = (64.0 * dot(hi.astype(BF), up) + dot(lo.astype(BF), up)) * UNIT
    feed = jnp.sqrt(1.0 - jnp.exp(2.0 * (v * UNIT)))
    return run, feed


def whole_step(
    gain_ref, x_hbm, new_hbm, cot_hbm, g_hbm, ld_ref, w_ref,
    nb, cb, dw_ref,
    xb, X, XT, gb, W, r_ref, proj, AT, GT, dec, runs, lead_s, tail_s, feed_s, runT, leadT, tailT,
    sc, dS, mix, dx, a_in, g_in, d_in, a_out, g_out, S_buf, G_buf, dB, dC, low, ng, side,
    part, r1buf, acc1, r2buf, acc2, r3buf,
    lsem, ss, rs, cs, cr, s1, r1, s2, r2, s3, r3, s4, r4, s5, r5,
    u1, v1, u2, v2, u3, v3,
):
    s = lax.axis_index("seq")
    f = lax.axis_index("fsdp")
    core = f % 2
    chip = f // 2
    sib = f + 1 - 2 * core

    loads = []
    for k, (a, b) in enumerate(((x_hbm, xb), (g_hbm, gb), (new_hbm, nb), (cot_hbm, cb))):
        c = pltpu.make_async_copy(a, b, lsem.at[k])
        c.start()
        loads.append(c)

    barrier = pltpu.get_barrier_semaphore()
    for k in range(1, 8):
        pl.semaphore_signal(
            barrier, inc=1, device_id=(s, (f + 2 * k) % FS), device_id_type=MESH
        )
        pl.semaphore_signal(
            barrier, inc=1, device_id=((s + k) % SEQ, f), device_id_type=MESH
        )
    pl.semaphore_signal(barrier, inc=1, device_id=(s, sib), device_id_type=MESH)
    pl.semaphore_wait(barrier, 15)

    def slot(i):
        return W.at[pl.ds(pl.multiple_of(i * 256, 256), 256)]

    def half(ref, p):
        return ref.at[:, pl.ds(p * N, N)]

    def to_peer(p, k):
        return pltpu.make_async_remote_copy(
            half(w_ref, p), half(slot(f), p), ss.at[p, k], rs.at[p, k],
            device_id=(s, (f + 2 * k) % FS), device_id_type=MESH,
        )

    def on(p, k):
        at = slot((f + FS - 2 * k) % FS)
        return pltpu.make_async_remote_copy(
            half(w_ref if k == 0 else at, p), half(at, p), cs.at[p, k], cr.at[p, k],
            device_id=(s, sib), device_id_type=MESH,
        )

    for p in range(2):
        for k in range(1, 8):
            to_peer(p, k).start()
        on(p, 0).start()
    W[pl.ds(pl.multiple_of(f * 256, 256), 256), :] = w_ref[...]

    run_rows, feed_rows = decays(ld_ref[...])
    runT[...] = run_rows
    leadT[...] = jnp.exp(run_rows)
    tailT[...] = feed_rows * jnp.exp(run_rows[:, T - 1 :] - run_rows)
    fill = jnp.zeros((N - H, T), F32)
    run = jnp.concatenate([run_rows, fill], axis=0).T[:, :H]
    feed = jnp.concatenate([feed_rows, fill], axis=0).T[:, :H]
    end = run[T - 1 : T, :]
    runs[...] = split(run, 3)
    lead_s[...] = split(jnp.exp(run), 2)
    tail_s[...] = split(feed * jnp.exp(end - run), 2)
    feed_s[...] = split(feed, 2)
    total = split(jnp.broadcast_to(jnp.exp(end), (8, H)), 3)
    for i in range(8):
        dec[i] = dot(total, pick(3, 4 * i, 4))

    loads[0].wait()

    def norm(i, _):
        rows = pl.ds(pl.multiple_of(i * 32, 32), 32)
        v = xb[rows, :].astype(F32)
        r = lax.rsqrt(jnp.mean(v * v, axis=1, keepdims=True) + EPS)
        r_ref[rows, :] = r
        X[rows, :] = (v * r).astype(BF)
        return 0

    lax.fori_loop(0, T // 32, norm, 0)

    def gathered(p):
        for k in range(1, 8):
            to_peer(p, k).wait_recv()
            on(p, k).start()
        for k in range(8):
            on(p, k).wait()

    def project(p):
        cols = slice(p * N, (p + 1) * N)
        for i in range(4):
            rows = slice(i * 128, (i + 1) * 128)
            proj[rows, cols] = dot(X[rows, :], W[:, cols]).astype(BF)
        return proj[:, cols].astype(F32).T

    def peer(src, dst, a, b, k):
        return pltpu.make_async_remote_copy(
            src, dst, a.at[k], b.at[k],
            device_id=((s + k) % SEQ, f), device_id_type=MESH,
        )

    def to_dec(k):
        return peer(dec.at[(s + k) % SEQ], d_in.at[s], s5, r5, k)

    def to_a(k):
        return peer(AT.at[(s + k) % SEQ], a_in.at[s], s1, r1, k)

    def to_g(k):
        return peer(GT.at[(s + k) % SEQ], g_in.at[s], s2, r2, k)

    def back_a(k):
        return peer(a_out.at[(s + k) % SEQ], S_buf.at[s], s3, r3, k)

    def back_g(k):
        return peer(g_out.at[(s + k) % SEQ], G_buf.at[s], s4, r4, k)

    gathered(0)
    side[...] = project(0)

    def make_a(k, _):
        i = (s + k) % SEQ
        for q in range(4):
            h = 4 * i + q
            bs = (side[...] * tailT[pl.ds(h, 1), :]).astype(BF)
            x = X[:, pl.ds(pl.multiple_of(h * N, N), N)]
            AT[i, :, q * N : (q + 1) * N] = dot(bs, x).astype(BF)

        @pl.when(k < SEQ)
        def _():
            to_dec(k).start()
            to_a(k).start()

        return 0

    lax.fori_loop(1, SEQ + 1, make_a, 0)
    gathered(1)
    loads[1].wait()
    side[...] = project(1) * RN

    def make_g(k, _):
        i = (s + k) % SEQ
        for q in range(4):
            h = 4 * i + q
            c = (side[...] * leadT[pl.ds(h, 1), :]).astype(BF)
            g = gb[:, pl.ds(pl.multiple_of(h * N, N), N)]
            GT[i, :, q * N : (q + 1) * N] = dot(c, g).astype(BF)

        @pl.when(k < SEQ)
        def _():
            to_g(k).start()

        return 0

    lax.fori_loop(1, SEQ + 1, make_g, 0)
    B = proj[:, :N]
    C = proj[:, N:]
    a_in[pl.ds(s, 1)] = AT[pl.ds(s, 1)]
    g_in[pl.ds(s, 1)] = GT[pl.ds(s, 1)]
    d_in[pl.ds(s, 1)] = dec[pl.ds(s, 1)]

    sc[...] = dot_nt(C, B) * RN
    dS[...] = jnp.zeros_like(dS)
    dB[...] = jnp.zeros_like(dB)
    dC[...] = jnp.zeros_like(dC)
    tri = lax.broadcasted_iota(jnp.int32, (N, N), 0) >= lax.broadcasted_iota(
        jnp.int32, (N, N), 1
    )

    def head(h, _):
        cols = pl.ds(pl.multiple_of(h * N, N), N)
        gain = gain_ref[h]
        run_b = dot(runs[...], pick(3, h, 1))
        feed_b = dot(feed_s[...], pick(2, h, 1))
        x = X[:, cols].astype(F32)
        XT[cols, :] = x.T.astype(BF)
        xf = (x * feed_b).astype(BF)
        g = gb[:, cols]
        row = runT[pl.ds(h, 1), :]
        w = [[None] * 4 for _ in range(4)]
        for i in range(4):
            ri = slice(i * N, (i + 1) * N)
            dP = dot_nt(g[ri], xf[: (i + 1) * N])
            for j in range(i + 1):
                rj = slice(j * N, (j + 1) * N)
                d = run_b[ri] - row[:, rj]
                if i == j:
                    e = jnp.where(tri, jnp.exp(jnp.minimum(d, 0.0)), 0.0)
                else:
                    e = jnp.exp(d)
                dS[ri, rj] += e * dP[:, rj]
                w[i][j] = (e * sc[ri, rj]).astype(BF)
            wi = w[i][0] if i == 0 else jnp.concatenate(w[i][: i + 1], axis=1)
            m = dot(wi, xf[: (i + 1) * N]) + gain * x[ri]
            mix[ri, cols] = m.astype(BF)
        for j in range(4):
            rj = slice(j * N, (j + 1) * N)
            wj = [w[i][j] for i in range(j, 4)]
            wj = wj[0] if len(wj) == 1 else jnp.concatenate(wj, axis=0)
            v = dot_tn(wj, g[j * N :]) * feed_b[rj] + gain * g[rj].astype(F32)
            dx[rj, cols] = v.astype(BF)
        return 0

    def wait_in(make):
        def one(k, _):
            make(k).wait()
            return 0

        lax.fori_loop(1, SEQ, one, 0)

    def start_back(make):
        def one(k, _):
            make(k).start()
            return 0

        lax.fori_loop(1, SEQ, one, 0)

    lax.fori_loop(0, HEADS_1, head, 0)

    wait_in(to_dec)
    wait_in(to_a)
    state = jnp.zeros((N, Q), F32)
    for j in range(SEQ):
        a_out[j] = state.astype(BF)
        if j < SEQ - 1:
            state = d_in[j, 0:1, :] * state + a_in[j].astype(F32)
    start_back(back_a)
    S_buf[pl.ds(s, 1)] = a_out[pl.ds(s, 1)]

    lax.fori_loop(HEADS_1, HEADS_2, head, 0)

    wait_in(to_g)
    state = jnp.zeros((N, Q), F32)
    for j in range(SEQ - 1, -1, -1):
        g_out[j] = state.astype(BF)
        if j > 0:
            state = d_in[j, 0:1, :] * state + g_in[j].astype(F32)
    start_back(back_g)
    G_buf[pl.ds(s, 1)] = g_out[pl.ds(s, 1)]

    lax.fori_loop(HEADS_2, H, head, 0)
    loads[2].wait()

    def to_sib(p, i):
        return pltpu.make_async_remote_copy(
            part.at[p, i, :, 1 - core], r1buf.at[p, i], u1.at[p, i], v1.at[p, i],
            device_id=(s, sib), device_id_type=MESH,
        )

    def to_chip(p, k):
        return pltpu.make_async_remote_copy(
            acc1.at[p, :, (chip + k) % 8], r2buf.at[p, k - 1], u2.at[p, k - 1], v2.at[p, k - 1],
            device_id=(s, (f + 2 * k) % FS), device_id_type=MESH,
        )

    def product(p):
        half_low = low[:, p * N : (p + 1) * N]

        def one(i, _):
            rows = pl.ds(pl.multiple_of(i * Q, Q), Q)
            v = dot(XT[rows, :], half_low).astype(BF)
            part[p, pl.ds(i, 1)] = v.reshape(1, 8, 2, 32, N)
            to_sib(p, i).start()
            return 0

        lax.fori_loop(0, SEQ, one, 0)

    def join(p):
        def one(i, _):
            to_sib(p, i).wait()
            mine = part[p, pl.ds(i, 1), :, pl.ds(core, 1)].reshape(8, 32, N)
            acc1[p, i] = (mine.astype(F32) + r1buf[p, i].astype(F32)).astype(BF)
            return 0

        lax.fori_loop(0, SEQ, one, 0)
        for k in range(1, 8):
            to_chip(p, k).start()

    def carried(k, _):
        @pl.when(k > 0)
        def _():
            back_a(k).wait()

        i = (s + SEQ - k) % SEQ
        cols = pl.ds(pl.multiple_of(i * Q, Q), Q)
        lead = dot(lead_s[...], pick(2, 4 * i, 4)) * RN
        S = S_buf[i]
        mixed = dot(C, S) * lead + mix[:, cols].astype(F32)
        nb[:, cols] = (nb[:, cols].astype(F32) - mixed).astype(BF)
        gs = (gb[:, cols].astype(F32) * lead).astype(BF)
        dC[...] += dot_nt(gs, S)
        return 0

    lax.fori_loop(0, SEQ, carried, 0)

    dSl = (dS[...] * RN).astype(BF)
    low[:, N:] = (dC[...] + dot(dSl, B)).astype(BF)
    product(1)
    dB[...] = dot_tn(dSl, C)
    join(1)

    def carried_back(k, _):
        @pl.when(k > 0)
        def _():
            back_g(k).wait()

        i = (s + SEQ - k) % SEQ
        cols = pl.ds(pl.multiple_of(i * Q, Q), Q)
        tail = dot(tail_s[...], pick(2, 4 * i, 4))
        G = G_buf[i]
        xs = (X[:, cols].astype(F32) * tail).astype(BF)
        dB[...] += dot_nt(xs, G)
        dx[:, cols] = (dot(B, G) * tail + dx[:, cols].astype(F32)).astype(BF)
        return 0

    lax.fori_loop(0, SEQ, carried_back, 0)
    low[:, :N] = dB[...].astype(BF)
    product(0)
    join(0)

    loads[3].wait()

    def normback(b, _):
        rows = pl.ds(pl.multiple_of(b * 128, 128), 128)
        lo = low[rows, :]
        xg = jnp.zeros((128, N), F32)
        for i in range(8):
            cols = slice(i * Q, (i + 1) * Q)
            v = dot_nt(lo, W[cols, :]) + dx[rows, cols].astype(F32)
            ng[:, cols] = v
            t = xb[rows, cols].astype(F32) * v
            xg += t[:, :N] + t[:, N : 2 * N] + t[:, 2 * N : 3 * N] + t[:, 3 * N :]
        r = r_ref[rows, :]
        back = r * r * r * (jnp.sum(xg, axis=1, keepdims=True) * (1.0 / D))
        for i in range(8):
            cols = slice(i * Q, (i + 1) * Q)
            v = r * ng[:, cols] - back * xb[rows, cols].astype(F32)
            cb[rows, cols] = (cb[rows, cols].astype(F32) + v).astype(BF)
        return 0

    lax.fori_loop(0, NB_1, normback, 0)

    for p in (1, 0):
        total = acc1[p, :, pl.ds(chip, 1)].reshape(8, 32, N).astype(F32)
        for k in range(1, 8):
            to_chip(p, k).wait()
            total += r2buf[p, k - 1].astype(F32)
        acc2[:, :, p * N : (p + 1) * N] = total.astype(BF)

    def to_seq(k):
        return pltpu.make_async_remote_copy(
            acc2.at[(s + k) % SEQ], r3buf.at[k - 1], u3.at[k - 1], v3.at[k - 1],
            device_id=((s + k) % SEQ, f), device_id_type=MESH,
        )

    for k in range(1, 8):
        to_seq(k).start()
    lax.fori_loop(NB_1, 4, normback, 0)
    for p in range(2):
        for k in range(1, 8):
            to_peer(p, k).wait_send()
    total = acc2[pl.ds(s, 1)].reshape(32, 256).astype(F32)
    for k in range(1, 8):
        to_seq(k).wait()
        total += r3buf[k - 1].astype(F32)
    dw_ref[...] = total * (T * SEQ * FS) ** (-0.5)


def shape(*dims, dtype=BF):
    return jax.ShapeDtypeStruct(dims, dtype)


HEADS_1 = 8
HEADS_2 = 22
NB_1 = 2
VM = pl.BlockSpec(memory_space=pltpu.VMEM)
ANY = pl.BlockSpec(memory_space=pl.ANY)
DMA = pltpu.SemaphoreType.DMA
LIMIT = 52 << 20


def shards(middle, newest, middle_cot, newest_cot, log_decay, weights, gain):
    def vm(*dims, dtype=BF):
        return pltpu.VMEM(dims, dtype)

    scratch = [
        vm(T, D), vm(T, D), vm(D, T), vm(T, D), vm(D, 2 * N), vm(T, 1, dtype=F32),
        vm(T, 2 * N), vm(SEQ, N, Q), vm(SEQ, N, Q), vm(SEQ, 8, Q, dtype=F32),
        vm(T, 3 * H), vm(T, 2 * H), vm(T, 2 * H), vm(T, 2 * H),
        vm(H, T, dtype=F32), vm(H, T, dtype=F32), vm(H, T, dtype=F32),
        vm(T, T, dtype=F32), vm(T, T, dtype=F32), vm(T, D), vm(T, D),
        vm(SEQ, N, Q), vm(SEQ, N, Q), vm(SEQ, 8, Q, dtype=F32),
        vm(SEQ, N, Q), vm(SEQ, N, Q), vm(SEQ, N, Q), vm(SEQ, N, Q),
        vm(T, N, dtype=F32), vm(T, N, dtype=F32), vm(T, 2 * N), vm(128, D, dtype=F32), vm(N, T, dtype=F32),
        vm(2, 8, 8, 2, 32, N), vm(2, 8, 8, 32, N), vm(2, 8, 8, 32, N), vm(2, 7, 8, 32, N),
        vm(8, 32, 256), vm(7, 32, 256),
        DMA((4,)), DMA((2, 8)), DMA((2, 8)), DMA((2, 8)), DMA((2, 8)),
    ] + [DMA((8,))] * 10 + [DMA((2, 8)), DMA((2, 8)), DMA((2, 7)), DMA((2, 7)), DMA((7,)), DMA((7,))]
    old, out, grad = pl.pallas_call(
        whole_step,
        name="step",
        out_shape=[vm(T, D), vm(T, D), vm(32, 2 * N, dtype=F32)],
        in_specs=[pl.BlockSpec(memory_space=pltpu.SMEM)] + [ANY] * 4 + [VM] * 2,
        out_specs=[VM, VM, VM],
        scratch_shapes=scratch,
        compiler_params=pltpu.CompilerParams(
            collective_id=0, has_side_effects=True, vmem_limit_bytes=LIMIT
        ),
    )(gain, middle[0], newest[0], middle_cot[0], newest_cot[0], log_decay[0].T, weights)
    return old[None], out[None], grad


def solution(mesh):
    return jax.shard_map(
        shards,
        mesh=mesh,
        in_specs=(P("fsdp", "seq", None),) * 5 + (P("fsdp", None), P()),
        out_specs=(P("fsdp", "seq", None), P("fsdp", "seq", None), P(("seq", "fsdp"), None)),
        check_vma=False,
    )
```

```python
import jax
import jax.numpy as jnp
from jax import lax
from jax.experimental import pallas as pl
from jax.experimental.pallas import tpu as pltpu
from jax.sharding import PartitionSpec as P

MESH = pl.DeviceIdType.MESH
F32 = jnp.float32
BF = jnp.bfloat16
T = 512
D = 4096
H = 32
N = 128
Q = 512
EPS = 1e-05
UNIT = 1.0 / 4096.0
RN = N ** (-0.5)
SEQ = 8
FS = 16


def dot(a, b):
    return jnp.dot(a, b, preferred_element_type=F32)


def dot_nt(a, b):
    return lax.dot_general(a, b, (((1,), (1,)), ((), ())), preferred_element_type=F32)


def dot_tn(a, b):
    return lax.dot_general(a, b, (((0,), (0,)), ((), ())), preferred_element_type=F32)


def split(v, parts):
    out = []
    for _ in range(parts):
        p = v.astype(BF)
        out.append(p)
        v = v - p.astype(F32)
    return jnp.concatenate(out, axis=1)


def pick(parts, head, heads):
    rows = lax.broadcasted_iota(jnp.int32, (parts * H, heads * N), 0)
    cols = lax.broadcasted_iota(jnp.int32, (parts * H, heads * N), 1)
    return (rows % H == head + cols // N).astype(F32).astype(BF)


def decays(ld):
    v = ld.astype(F32)
    hi = jnp.floor(v * (1.0 / 64.0))
    lo = v - hi * 64.0
    up = lax.broadcasted_iota(jnp.int32, (T, T), 0) <= lax.broadcasted_iota(
        jnp.int32, (T, T), 1
    )
    up = up.astype(F32).astype(BF)
    run = (64.0 * dot(hi.astype(BF), up) + dot(lo.astype(BF), up)) * UNIT
    feed = jnp.sqrt(1.0 - jnp.exp(2.0 * (v * UNIT)))
    return run, feed


def whole_step(
    gain_ref, x_hbm, new_hbm, cot_hbm, g_hbm, ld_ref, w_ref,
    nb, cb, dw_ref,
    xb, X, XT, gb, W, r_ref, proj, AT, GT, dec, runs, lead_s, tail_s, feed_s, runT, leadT, tailT,
    sc, dS, mix, dx, a_in, g_in, d_in, a_out, g_out, S_buf, G_buf, dB, dC, low, ng, side,
    part, r1buf, acc1, r2buf, acc2, r3buf,
    lsem, ss, rs, cs, cr, s1, r1, s2, r2, s3, r3, s4, r4, s5, r5,
    u1, v1, u2, v2, u3, v3,
):
    s = lax.axis_index("seq")
    f = lax.axis_index("fsdp")
    core = f % 2
    side_x = f // 8
    other = (f + 8) % FS
    y = (f // 2) % 4
    sib = f + 1 - 2 * core

    loads = []
    for k, (a, b) in enumerate(((x_hbm, xb), (g_hbm, gb), (new_hbm, nb), (cot_hbm, cb))):
        loads.append(pltpu.make_async_copy(a, b, lsem.at[k]))
    loads[0].start()

    barrier = pltpu.get_barrier_semaphore()
    def along_y(j):
        return side_x * 8 + (f % 8 + 2 * j) % 8

    def greet(where):
        pl.semaphore_signal(barrier, inc=1, device_id=where, device_id_type=MESH)

    for j in range(1, 4):
        greet((s, along_y(j)))
    for k in range(1, SEQ):
        greet(((s + k) % SEQ, f))
        greet(((s + k) % SEQ, other))
    greet((s, other))
    greet((s, sib))
    pl.semaphore_wait(barrier, 19)

    def slot(i):
        return W.at[pl.ds(pl.multiple_of(i * 256, 256), 256)]

    def half(ref, p):
        return ref.at[:, pl.ds(p * N, N)]

    def to_peer(p, m):
        if m == 4:
            a, b, to = w_ref, slot(f), other
        elif m < 4:
            a, b, to = w_ref, slot(f), along_y(m)
        else:
            a, b, to = slot(other), slot(other), along_y(m - 4)
        return pltpu.make_async_remote_copy(
            half(a, p), half(b, p), ss.at[p, m], rs.at[p, m],
            device_id=(s, to), device_id_type=MESH,
        )

    def on(p, m):
        at = slot(((side_x + m // 4) % 2) * 8 + (f % 8 + 8 - 2 * (m % 4)) % 8)
        return pltpu.make_async_remote_copy(
            half(w_ref if m == 0 else at, p), half(at, p), cs.at[p, m], cr.at[p, m],
            device_id=(s, sib), device_id_type=MESH,
        )

    def first_sends(p):
        for m in (4, 1, 2, 3):
            to_peer(p, m).start()

    def forward(p):
        to_peer(p, 4).wait_recv()
        for m in (5, 6, 7):
            to_peer(p, m).start()
        on(p, 4).start()

    first_sends(0)
    for p in range(2):
        on(p, 0).start()
    loads[1].start()
    W[pl.ds(pl.multiple_of(f * 256, 256), 256), :] = w_ref[...]

    run_rows, feed_rows = decays(ld_ref[...])
    runT[...] = run_rows
    leadT[...] = jnp.exp(run_rows)
    tailT[...] = feed_rows * jnp.exp(run_rows[:, T - 1 :] - run_rows)
    fill = jnp.zeros((N - H, T), F32)
    run = jnp.concatenate([run_rows, fill], axis=0).T[:, :H]
    feed = jnp.concatenate([feed_rows, fill], axis=0).T[:, :H]
    end = run[T - 1 : T, :]
    runs[...] = split(run, 3)
    lead_s[...] = split(jnp.exp(run), 2)
    tail_s[...] = split(feed * jnp.exp(end - run), 2)
    feed_s[...] = split(feed, 2)
    total = split(jnp.broadcast_to(jnp.exp(end), (8, H)), 3)
    for i in range(8):
        dec[i] = dot(total, pick(3, 4 * i, 4))

    forward(0)
    loads[0].wait()

    def norm(i, _):
        rows = pl.ds(pl.multiple_of(i * 32, 32), 32)
        v = xb[rows, :].astype(F32)
        r = lax.rsqrt(jnp.mean(v * v, axis=1, keepdims=True) + EPS)
        r_ref[rows, :] = r
        X[rows, :] = (v * r).astype(BF)
        return 0

    lax.fori_loop(0, T // 32, norm, 0)
    for k in range(1, 8):
        to_peer(0, k).wait_send()
    first_sends(1)

    def gathered(p):
        for m in (1, 2, 3, 5, 6, 7):
            to_peer(p, m).wait_recv()
            on(p, m).start()
        for k in range(8):
            on(p, k).wait()

    def project(p):
        cols = slice(p * N, (p + 1) * N)
        for i in range(4):
            rows = slice(i * 128, (i + 1) * 128)
            proj[rows, cols] = dot(X[rows, :], W[:, cols]).astype(BF)
        return proj[:, cols].astype(F32).T

    def peer(src, dst, a, b, k):
        return pltpu.make_async_remote_copy(
            src, dst, a.at[k], b.at[k],
            device_id=((s + k) % SEQ, f), device_id_type=MESH,
        )

    def to_dec(k):
        return peer(dec.at[(s + k) % SEQ], d_in.at[s], s5, r5, k)

    def to_a(k):
        return peer(AT.at[(s + k) % SEQ], a_in.at[s], s1, r1, k)

    def to_g(k):
        return peer(GT.at[(s + k) % SEQ], g_in.at[s], s2, r2, k)

    def back_a(k):
        return peer(a_out.at[(s + k) % SEQ], S_buf.at[s], s3, r3, k)

    def back_g(k):
        return peer(g_out.at[(s + k) % SEQ], G_buf.at[s], s4, r4, k)

    gathered(0)
    side[...] = project(0)
    forward(1)

    def make_a(k, _):
        i = (s + k) % SEQ
        for q in range(4):
            h = 4 * i + q
            bs = (side[...] * tailT[pl.ds(h, 1), :]).astype(BF)
            x = X[:, pl.ds(pl.multiple_of(h * N, N), N)]
            AT[i, :, q * N : (q + 1) * N] = dot(bs, x).astype(BF)

        @pl.when(k < SEQ)
        def _():
            to_dec(k).start()
            to_a(k).start()

        return 0

    lax.fori_loop(1, SEQ + 1, make_a, 0)
    gathered(1)
    loads[1].wait()
    side[...] = project(1) * RN

    def make_g(k, _):
        i = (s + k) % SEQ
        for q in range(4):
            h = 4 * i + q
            c = (side[...] * leadT[pl.ds(h, 1), :]).astype(BF)
            g = gb[:, pl.ds(pl.multiple_of(h * N, N), N)]
            GT[i, :, q * N : (q + 1) * N] = dot(c, g).astype(BF)
        return 0

    lax.fori_loop(1, SEQ + 1, make_g, 0)
    loads[2].start()
    loads[3].start()
    B = proj[:, :N]
    C = proj[:, N:]
    a_in[pl.ds(s, 1)] = AT[pl.ds(s, 1)]
    g_in[pl.ds(s, 1)] = GT[pl.ds(s, 1)]
    d_in[pl.ds(s, 1)] = dec[pl.ds(s, 1)]

    sc[...] = dot_nt(C, B) * RN
    dS[...] = jnp.zeros_like(dS)
    dB[...] = jnp.zeros_like(dB)
    dC[...] = jnp.zeros_like(dC)
    tri = lax.broadcasted_iota(jnp.int32, (N, N), 0) >= lax.broadcasted_iota(
        jnp.int32, (N, N), 1
    )

    def head(h, _):
        cols = pl.ds(pl.multiple_of(h * N, N), N)
        gain = gain_ref[h]
        run_b = dot(runs[...], pick(3, h, 1))
        feed_b = dot(feed_s[...], pick(2, h, 1))
        x = X[:, cols].astype(F32)
        XT[cols, :] = x.T.astype(BF)
        xf = (x * feed_b).astype(BF)
        g = gb[:, cols]
        row = runT[pl.ds(h, 1), :]
        w = [[None] * 4 for _ in range(4)]
        for i in range(4):
            ri = slice(i * N, (i + 1) * N)
            dP = dot_nt(g[ri], xf[: (i + 1) * N])
            for j in range(i + 1):
                rj = slice(j * N, (j + 1) * N)
                d = run_b[ri] - row[:, rj]
                if i == j:
                    e = jnp.where(tri, jnp.exp(jnp.minimum(d, 0.0)), 0.0)
                else:
                    e = jnp.exp(d)
                dS[ri, rj] += e * dP[:, rj]
                w[i][j] = (e * sc[ri, rj]).astype(BF)
            wi = w[i][0] if i == 0 else jnp.concatenate(w[i][: i + 1], axis=1)
            m = dot(wi, xf[: (i + 1) * N]) + gain * x[ri]
            mix[ri, cols] = m.astype(BF)
        for j in range(4):
            rj = slice(j * N, (j + 1) * N)
            wj = [w[i][j] for i in range(j, 4)]
            wj = wj[0] if len(wj) == 1 else jnp.concatenate(wj, axis=0)
            v = dot_tn(wj, g[j * N :]) * feed_b[rj] + gain * g[rj].astype(F32)
            dx[rj, cols] = v.astype(BF)
        return 0

    def wait_in(make):
        def one(k, _):
            make(k).wait()
            return 0

        lax.fori_loop(1, SEQ, one, 0)

    def start_back(make):
        def one(k, _):
            make(k).start()
            return 0

        lax.fori_loop(1, SEQ, one, 0)

    def then(first, second, base):
        def one(k, _):
            first(k).wait_send()
            second(k).start()
            head(base + k - 1, 0)
            return 0

        lax.fori_loop(1, SEQ, one, 0)

    def wait_recv(make):
        def one(k, _):
            make(k).wait_recv()
            return 0

        lax.fori_loop(1, SEQ, one, 0)

    then(to_a, to_g, 0)
    lax.fori_loop(SEQ - 1, HEADS_1, head, 0)

    wait_in(to_dec)
    wait_recv(to_a)
    state = jnp.zeros((N, Q), F32)
    for j in range(SEQ):
        a_out[j] = state.astype(BF)
        if j < SEQ - 1:
            state = d_in[j, 0:1, :] * state + a_in[j].astype(F32)
    start_back(back_a)
    S_buf[pl.ds(s, 1)] = a_out[pl.ds(s, 1)]

    lax.fori_loop(HEADS_1, HEADS_2, head, 0)

    wait_in(to_g)
    state = jnp.zeros((N, Q), F32)
    for j in range(SEQ - 1, -1, -1):
        g_out[j] = state.astype(BF)
        if j > 0:
            state = d_in[j, 0:1, :] * state + g_in[j].astype(F32)
    then(back_a, back_g, HEADS_2)
    G_buf[pl.ds(s, 1)] = g_out[pl.ds(s, 1)]

    lax.fori_loop(HEADS_2 + SEQ - 1, H, head, 0)
    loads[2].wait()

    def to_sib(p, i):
        return pltpu.make_async_remote_copy(
            part.at[p, i, :, 1 - core], r1buf.at[p, i], u1.at[p, i], v1.at[p, i],
            device_id=(s, sib), device_id_type=MESH,
        )

    def to_y(p, j):
        return pltpu.make_async_remote_copy(
            acc1.at[p, :, :, (y + j) % 4], r2buf.at[p, j - 1], u2.at[p, j - 1], v2.at[p, j - 1],
            device_id=(s, along_y(j)), device_id_type=MESH,
        )

    def product(p):
        half_low = low[:, p * N : (p + 1) * N]

        def one(i, _):
            rows = pl.ds(pl.multiple_of(i * Q, Q), Q)
            v = dot(XT[rows, :], half_low).astype(BF)
            part[p, pl.ds(i, 1)] = v.reshape(1, 8, 2, 32, N)
            to_sib(p, i).start()
            return 0

        lax.fori_loop(0, SEQ, one, 0)

    def join(p):
        def one(i, _):
            to_sib(p, i).wait()
            mine = part[p, pl.ds(i, 1), :, pl.ds(core, 1)].reshape(8, 32, N)
            v = (mine.astype(F32) + r1buf[p, i].astype(F32)).astype(BF)
            acc1[p, i] = v.reshape(2, 4, 32, N)
            return 0

        lax.fori_loop(0, SEQ, one, 0)
        for j in range(1, 4):
            to_y(p, j).start()

    def carried(k, _):
        @pl.when(k > 0)
        def _():
            back_a(k).wait_recv()

        i = (s + SEQ - k) % SEQ
        cols = pl.ds(pl.multiple_of(i * Q, Q), Q)
        lead = dot(lead_s[...], pick(2, 4 * i, 4)) * RN
        S = S_buf[i]
        mixed = dot(C, S) * lead + mix[:, cols].astype(F32)
        nb[:, cols] = (nb[:, cols].astype(F32) - mixed).astype(BF)
        gs = (gb[:, cols].astype(F32) * lead).astype(BF)
        dC[...] += dot_nt(gs, S)
        return 0

    lax.fori_loop(0, SEQ, carried, 0)

    dSl = (dS[...] * RN).astype(BF)
    low[:, N:] = (dC[...] + dot(dSl, B)).astype(BF)
    product(1)
    dB[...] = dot_tn(dSl, C)
    join(1)

    def carried_back(k, _):
        @pl.when(k > 0)
        def _():
            back_g(k).wait()

        i = (s + SEQ - k) % SEQ
        cols = pl.ds(pl.multiple_of(i * Q, Q), Q)
        tail = dot(tail_s[...], pick(2, 4 * i, 4))
        G = G_buf[i]
        xs = (X[:, cols].astype(F32) * tail).astype(BF)
        dB[...] += dot_nt(xs, G)
        dx[:, cols] = (dot(B, G) * tail + dx[:, cols].astype(F32)).astype(BF)
        return 0

    lax.fori_loop(0, SEQ, carried_back, 0)
    low[:, :N] = dB[...].astype(BF)
    product(0)
    join(0)

    loads[3].wait()

    def normback(b, _):
        rows = pl.ds(pl.multiple_of(b * 128, 128), 128)
        lo = low[rows, :]
        xg = jnp.zeros((128, N), F32)
        for i in range(8):
            cols = slice(i * Q, (i + 1) * Q)
            v = dot_nt(lo, W[cols, :]) + dx[rows, cols].astype(F32)
            ng[:, cols] = v
            t = xb[rows, cols].astype(F32) * v
            xg += t[:, :N] + t[:, N : 2 * N] + t[:, 2 * N : 3 * N] + t[:, 3 * N :]
        r = r_ref[rows, :]
        back = r * r * r * (jnp.sum(xg, axis=1, keepdims=True) * (1.0 / D))
        for i in range(8):
            cols = slice(i * Q, (i + 1) * Q)
            v = r * ng[:, cols] - back * xb[rows, cols].astype(F32)
            cb[rows, cols] = (cb[rows, cols].astype(F32) + v).astype(BF)
        return 0

    lax.fori_loop(0, NB_1, normback, 0)

    for p in (1, 0):
        total = acc1[p, :, :, pl.ds(y, 1)].reshape(8, 2, 32, N).astype(F32)
        for j in range(1, 4):
            to_y(p, j).wait()
            total += r2buf[p, j - 1].astype(F32)
        acc2[:, :, :, p * N : (p + 1) * N] = total.astype(BF)

    def to_end(m):
        place, row = (side_x + m // 8) % 2, (s + m % 8) % SEQ
        return pltpu.make_async_remote_copy(
            acc2.at[row, place], r3buf.at[m - 1], u3.at[m - 1], v3.at[m - 1],
            device_id=(row, place * 8 + f % 8), device_id_type=MESH,
        )

    for m in range(1, 16):
        to_end(m).start()
    lax.fori_loop(NB_1, 4, normback, 0)
    for k in range(1, 8):
        to_peer(1, k).wait_send()
    total = acc2[pl.ds(s, 1), pl.ds(side_x, 1)].reshape(32, 256).astype(F32)
    for m in range(1, 16):
        to_end(m).wait()
        total += r3buf[m - 1].astype(F32)
    dw_ref[...] = total * (T * SEQ * FS) ** (-0.5)


def store(old_ref, grad_ref, dw_ref, old_hbm, grad_hbm, dw_hbm, sem):
    copies = []
    for p in range(4):
        rows = pl.ds(p * 128, 128)
        for n, (a, b) in enumerate(((old_ref, old_hbm), (grad_ref, grad_hbm))):
            copies.append(pltpu.make_async_copy(a.at[rows], b.at[rows], sem.at[2 * p + n]))
    copies.append(pltpu.make_async_copy(dw_ref, dw_hbm, sem.at[8]))
    for c in copies:
        c.start()
    for c in copies:
        c.wait()


def shape(*dims, dtype=BF):
    return jax.ShapeDtypeStruct(dims, dtype)


HEADS_1 = 9
HEADS_2 = 22
NB_1 = 2
VM = pl.BlockSpec(memory_space=pltpu.VMEM)
ANY = pl.BlockSpec(memory_space=pl.ANY)
DMA = pltpu.SemaphoreType.DMA
LIMIT = 52 << 20


def shards(middle, newest, middle_cot, newest_cot, log_decay, weights, gain):
    def vm(*dims, dtype=BF):
        return pltpu.VMEM(dims, dtype)

    scratch = [
        vm(T, D), vm(T, D), vm(D, T), vm(T, D), vm(D, 2 * N), vm(T, 1, dtype=F32),
        vm(T, 2 * N), vm(SEQ, N, Q), vm(SEQ, N, Q), vm(SEQ, 8, Q, dtype=F32),
        vm(T, 3 * H), vm(T, 2 * H), vm(T, 2 * H), vm(T, 2 * H),
        vm(H, T, dtype=F32), vm(H, T, dtype=F32), vm(H, T, dtype=F32),
        vm(T, T, dtype=F32), vm(T, T, dtype=F32), vm(T, D), vm(T, D),
        vm(SEQ, N, Q), vm(SEQ, N, Q), vm(SEQ, 8, Q, dtype=F32),
        vm(SEQ, N, Q), vm(SEQ, N, Q), vm(SEQ, N, Q), vm(SEQ, N, Q),
        vm(T, N, dtype=F32), vm(T, N, dtype=F32), vm(T, 2 * N), vm(128, D, dtype=F32), vm(N, T, dtype=F32),
        vm(2, 8, 8, 2, 32, N), vm(2, 8, 8, 32, N), vm(2, 8, 2, 4, 32, N), vm(2, 3, 8, 2, 32, N),
        vm(8, 2, 32, 256), vm(15, 32, 256),
        DMA((4,)), DMA((2, 8)), DMA((2, 8)), DMA((2, 8)), DMA((2, 8)),
    ] + [DMA((8,))] * 10 + [DMA((2, 8)), DMA((2, 8)), DMA((2, 3)), DMA((2, 3)), DMA((15,)), DMA((15,))]
    old, out, grad = pl.pallas_call(
        whole_step,
        name="step",
        out_shape=[vm(T, D), vm(T, D), vm(32, 2 * N, dtype=F32)],
        in_specs=[pl.BlockSpec(memory_space=pltpu.SMEM)] + [ANY] * 4 + [VM] * 2,
        out_specs=[VM, VM, VM],
        scratch_shapes=scratch,
        compiler_params=pltpu.CompilerParams(
            collective_id=0, has_side_effects=True, vmem_limit_bytes=LIMIT
        ),
    )(gain, middle[0], newest[0], middle_cot[0], newest_cot[0], log_decay[0].T, weights)
    held = [pltpu.with_memory_space_constraint(a, pltpu.VMEM) for a in (old, out, grad)]
    old, out, grad = pl.pallas_call(
        store,
        name="store",
        out_shape=[shape(T, D), shape(T, D), shape(32, 2 * N, dtype=F32)],
        in_specs=[VM] * 3,
        out_specs=[ANY] * 3,
        scratch_shapes=[DMA((9,))],
        compiler_params=pltpu.CompilerParams(vmem_limit_bytes=4 << 20),
    )(*held)
    return old[None], out[None], grad


def solution(mesh):
    return jax.shard_map(
        shards,
        mesh=mesh,
        in_specs=(P("fsdp", "seq", None),) * 5 + (P("fsdp", None), P()),
        out_specs=(P("fsdp", "seq", None), P("fsdp", "seq", None), P(("seq", "fsdp"), None)),
        check_vma=False,
    )
```

```python
import jax
import jax.numpy as jnp
from jax import lax
from jax.experimental import pallas as pl
from jax.experimental.pallas import tpu as pltpu
from jax.sharding import PartitionSpec as P

MESH = pl.DeviceIdType.MESH
F32 = jnp.float32
BF = jnp.bfloat16
T = 512
D = 4096
H = 32
N = 128
Q = 512
EPS = 1e-05
UNIT = 1.0 / 4096.0
RN = N ** (-0.5)
SEQ = 8
FS = 16


def dot(a, b):
    return jnp.dot(a, b, preferred_element_type=F32)


def dot_nt(a, b):
    return lax.dot_general(a, b, (((1,), (1,)), ((), ())), preferred_element_type=F32)


def dot_tn(a, b):
    return lax.dot_general(a, b, (((0,), (0,)), ((), ())), preferred_element_type=F32)


def split(v, parts):
    out = []
    for _ in range(parts):
        p = v.astype(BF)
        out.append(p)
        v = v - p.astype(F32)
    return jnp.concatenate(out, axis=1)


def pick(parts, head, heads):
    rows = lax.broadcasted_iota(jnp.int32, (parts * H, heads * N), 0)
    cols = lax.broadcasted_iota(jnp.int32, (parts * H, heads * N), 1)
    return (rows % H == head + cols // N).astype(F32).astype(BF)


def decays(ld):
    v = ld.astype(F32)
    hi = jnp.floor(v * (1.0 / 64.0))
    lo = v - hi * 64.0
    up = lax.broadcasted_iota(jnp.int32, (T, T), 0) <= lax.broadcasted_iota(
        jnp.int32, (T, T), 1
    )
    up = up.astype(F32).astype(BF)
    run = (64.0 * dot(hi.astype(BF), up) + dot(lo.astype(BF), up)) * UNIT
    feed = jnp.sqrt(1.0 - jnp.exp(2.0 * (v * UNIT)))
    return run, feed


def whole_step(
    gain_ref, x_hbm, new_hbm, cot_hbm, g_hbm, ld_ref, w_ref,
    nb, cb, dw_ref,
    xb, X, XT, gb, W, r_ref, proj, AT, GT, dec, runs, lead_s, tail_s, feed_s, runT, leadT, tailT,
    sc, dS, mix, dx, a_in, g_in, d_in, a_out, g_out, S_buf, G_buf, dB, dC, low, ng, side,
    part, r1buf, acc1, r2buf, acc2, r3buf,
    lsem, ss, rs, cs, cr, s1, r1, s2, r2, s3, r3, s4, r4, s5, r5,
    u1, v1, u2, v2, u3, v3,
):
    s = lax.axis_index("seq")
    f = lax.axis_index("fsdp")
    core = f % 2
    side_x = f // 8
    other = (f + 8) % FS
    y = (f // 2) % 4
    sib = f + 1 - 2 * core

    loads = []
    for k, (a, b) in enumerate(((x_hbm, xb), (g_hbm, gb), (new_hbm, nb), (cot_hbm, cb))):
        loads.append(pltpu.make_async_copy(a, b, lsem.at[k]))
    loads[0].start()

    barrier = pltpu.get_barrier_semaphore()
    def along_y(j):
        return side_x * 8 + (f % 8 + 2 * j) % 8

    def greet(where):
        pl.semaphore_signal(barrier, inc=1, device_id=where, device_id_type=MESH)

    for j in range(1, 4):
        greet((s, along_y(j)))
    for k in range(1, SEQ):
        greet(((s + k) % SEQ, f))
        greet(((s + k) % SEQ, other))
    greet((s, other))
    greet((s, sib))
    pl.semaphore_wait(barrier, 19)

    def slot(i):
        return W.at[pl.ds(pl.multiple_of(i * 256, 256), 256)]

    def half(ref, p):
        return ref.at[:, pl.ds(p * N, N)]

    def to_peer(p, m):
        if m == 4:
            a, b, to = w_ref, slot(f), other
        elif m < 4:
            a, b, to = w_ref, slot(f), along_y(m)
        else:
            a, b, to = slot(other), slot(other), along_y(m - 4)
        return pltpu.make_async_remote_copy(
            half(a, p), half(b, p), ss.at[p, m], rs.at[p, m],
            device_id=(s, to), device_id_type=MESH,
        )

    def on(p, m):
        at = slot(((side_x + m // 4) % 2) * 8 + (f % 8 + 8 - 2 * (m % 4)) % 8)
        return pltpu.make_async_remote_copy(
            half(w_ref if m == 0 else at, p), half(at, p), cs.at[p, m], cr.at[p, m],
            device_id=(s, sib), device_id_type=MESH,
        )

    def first_sends(p):
        for m in (4, 1, 2, 3):
            to_peer(p, m).start()

    def forward(p):
        to_peer(p, 4).wait_recv()
        for m in (5, 6, 7):
            to_peer(p, m).start()
        on(p, 4).start()

    first_sends(0)
    for p in range(2):
        on(p, 0).start()
    loads[1].start()
    W[pl.ds(pl.multiple_of(f * 256, 256), 256), :] = w_ref[...]

    run_rows, feed_rows = decays(ld_ref[...])
    runT[...] = run_rows
    leadT[...] = jnp.exp(run_rows)
    tailT[...] = feed_rows * jnp.exp(run_rows[:, T - 1 :] - run_rows)
    fill = jnp.zeros((N - H, T), F32)
    run = jnp.concatenate([run_rows, fill], axis=0).T[:, :H]
    feed = jnp.concatenate([feed_rows, fill], axis=0).T[:, :H]
    end = run[T - 1 : T, :]
    runs[...] = split(run, 3)
    lead_s[...] = split(jnp.exp(run), 2)
    tail_s[...] = split(feed * jnp.exp(end - run), 2)
    feed_s[...] = split(feed, 2)
    total = split(jnp.broadcast_to(jnp.exp(end), (8, H)), 3)
    for i in range(8):
        dec[i] = dot(total, pick(3, 4 * i, 4))

    forward(0)
    loads[0].wait()

    def norm(i, _):
        rows = pl.ds(pl.multiple_of(i * 32, 32), 32)
        v = xb[rows, :].astype(F32)
        r = lax.rsqrt(jnp.mean(v * v, axis=1, keepdims=True) + EPS)
        r_ref[rows, :] = r
        X[rows, :] = (v * r).astype(BF)
        return 0

    lax.fori_loop(0, T // 32, norm, 0)
    for k in range(1, 8):
        to_peer(0, k).wait_send()
    first_sends(1)

    def gathered(p):
        for m in (1, 2, 3, 5, 6, 7):
            to_peer(p, m).wait_recv()
            on(p, m).start()
        for k in range(8):
            on(p, k).wait()

    def project(p):
        cols = slice(p * N, (p + 1) * N)
        for i in range(4):
            rows = slice(i * 128, (i + 1) * 128)
            proj[rows, cols] = dot(X[rows, :], W[:, cols]).astype(BF)
        return proj[:, cols].astype(F32).T

    def peer(src, dst, a, b, k):
        return pltpu.make_async_remote_copy(
            src, dst, a.at[k], b.at[k],
            device_id=((s + k) % SEQ, f), device_id_type=MESH,
        )

    def to_dec(k):
        return peer(dec.at[(s + k) % SEQ], d_in.at[s], s5, r5, k)

    def to_a(k):
        return peer(AT.at[(s + k) % SEQ], a_in.at[s], s1, r1, k)

    def to_g(k):
        return peer(GT.at[(s + k) % SEQ], g_in.at[s], s2, r2, k)

    def back_a(k):
        return peer(a_out.at[(s + k) % SEQ], S_buf.at[s], s3, r3, k)

    def back_g(k):
        return peer(g_out.at[(s + k) % SEQ], G_buf.at[s], s4, r4, k)

    gathered(0)
    side[...] = project(0)
    forward(1)

    def make_a(k, _):
        i = (s + k) % SEQ
        for q in range(4):
            h = 4 * i + q
            bs = (side[...] * tailT[pl.ds(h, 1), :]).astype(BF)
            x = X[:, pl.ds(pl.multiple_of(h * N, N), N)]
            AT[i, :, q * N : (q + 1) * N] = dot(bs, x).astype(BF)

        @pl.when(k < SEQ)
        def _():
            to_dec(k).start()
            to_a(k).start()

        return 0

    lax.fori_loop(1, SEQ + 1, make_a, 0)
    gathered(1)
    loads[1].wait()
    side[...] = project(1) * RN

    def make_g(k, _):
        i = (s + k) % SEQ
        for q in range(4):
            h = 4 * i + q
            c = (side[...] * leadT[pl.ds(h, 1), :]).astype(BF)
            g = gb[:, pl.ds(pl.multiple_of(h * N, N), N)]
            GT[i, :, q * N : (q + 1) * N] = dot(c, g).astype(BF)
        return 0

    lax.fori_loop(1, SEQ + 1, make_g, 0)
    loads[2].start()
    loads[3].start()
    B = proj[:, :N]
    C = proj[:, N:]
    a_in[pl.ds(s, 1)] = AT[pl.ds(s, 1)]
    g_in[pl.ds(s, 1)] = GT[pl.ds(s, 1)]
    d_in[pl.ds(s, 1)] = dec[pl.ds(s, 1)]

    sc[...] = dot_nt(C, B) * RN
    dS[...] = jnp.zeros_like(dS)
    dB[...] = jnp.zeros_like(dB)
    dC[...] = jnp.zeros_like(dC)
    tri = lax.broadcasted_iota(jnp.int32, (N, N), 0) >= lax.broadcasted_iota(
        jnp.int32, (N, N), 1
    )

    def head(h, _):
        cols = pl.ds(pl.multiple_of(h * N, N), N)
        gain = gain_ref[h]
        run_b = dot(runs[...], pick(3, h, 1))
        feed_b = dot(feed_s[...], pick(2, h, 1))
        x = X[:, cols].astype(F32)
        XT[cols, :] = x.T.astype(BF)
        xf = (x * feed_b).astype(BF)
        g = gb[:, cols]
        row = runT[pl.ds(h, 1), :]
        w = [[None] * 4 for _ in range(4)]
        for i in range(4):
            ri = slice(i * N, (i + 1) * N)
            dP = dot_nt(g[ri], xf[: (i + 1) * N])
            for j in range(i + 1):
                rj = slice(j * N, (j + 1) * N)
                d = run_b[ri] - row[:, rj]
                if i == j:
                    e = jnp.where(tri, jnp.exp(jnp.minimum(d, 0.0)), 0.0)
                else:
                    e = jnp.exp(d)
                dS[ri, rj] += e * dP[:, rj]
                w[i][j] = (e * sc[ri, rj]).astype(BF)
            wi = w[i][0] if i == 0 else jnp.concatenate(w[i][: i + 1], axis=1)
            m = dot(wi, xf[: (i + 1) * N]) + gain * x[ri]
            mix[ri, cols] = m.astype(BF)
        for j in range(4):
            rj = slice(j * N, (j + 1) * N)
            wj = [w[i][j] for i in range(j, 4)]
            wj = wj[0] if len(wj) == 1 else jnp.concatenate(wj, axis=0)
            v = dot_tn(wj, g[j * N :]) * feed_b[rj] + gain * g[rj].astype(F32)
            dx[rj, cols] = v.astype(BF)
        return 0

    def wait_in(make):
        def one(k, _):
            make(k).wait()
            return 0

        lax.fori_loop(1, SEQ, one, 0)

    def start_back(make):
        def one(k, _):
            make(k).start()
            return 0

        lax.fori_loop(1, SEQ, one, 0)

    def then(first, second, base):
        def one(k, _):
            first(k).wait_send()
            second(k).start()
            head(base + k - 1, 0)
            return 0

        lax.fori_loop(1, SEQ, one, 0)

    def wait_recv(make):
        def one(k, _):
            make(k).wait_recv()
            return 0

        lax.fori_loop(1, SEQ, one, 0)

    then(to_a, to_g, 0)
    lax.fori_loop(SEQ - 1, HEADS_1, head, 0)

    wait_in(to_dec)
    wait_recv(to_a)
    state = jnp.zeros((N, Q), F32)
    for j in range(SEQ):
        a_out[j] = state.astype(BF)
        if j < SEQ - 1:
            state = d_in[j, 0:1, :] * state + a_in[j].astype(F32)
    start_back(back_a)
    S_buf[pl.ds(s, 1)] = a_out[pl.ds(s, 1)]

    lax.fori_loop(HEADS_1, HEADS_2, head, 0)

    wait_in(to_g)
    state = jnp.zeros((N, Q), F32)
    for j in range(SEQ - 1, -1, -1):
        g_out[j] = state.astype(BF)
        if j > 0:
            state = d_in[j, 0:1, :] * state + g_in[j].astype(F32)
    then(back_a, back_g, HEADS_2)
    G_buf[pl.ds(s, 1)] = g_out[pl.ds(s, 1)]

    lax.fori_loop(HEADS_2 + SEQ - 1, H, head, 0)
    loads[2].wait()

    def to_sib(p, i):
        return pltpu.make_async_remote_copy(
            part.at[p, i, :, 1 - core], r1buf.at[p, i], u1.at[p, i], v1.at[p, i],
            device_id=(s, sib), device_id_type=MESH,
        )

    def to_y(p, j):
        return pltpu.make_async_remote_copy(
            acc1.at[p, :, :, (y + j) % 4], r2buf.at[p, j - 1], u2.at[p, j - 1], v2.at[p, j - 1],
            device_id=(s, along_y(j)), device_id_type=MESH,
        )

    def product(p):
        half_low = low[:, p * N : (p + 1) * N]

        def one(i, _):
            rows = pl.ds(pl.multiple_of(i * Q, Q), Q)
            v = dot(XT[rows, :], half_low).astype(BF)
            part[p, pl.ds(i, 1)] = v.reshape(1, 8, 2, 32, N)
            to_sib(p, i).start()
            return 0

        lax.fori_loop(0, SEQ, one, 0)

    def join(p):
        def one(i, _):
            to_sib(p, i).wait()
            mine = part[p, pl.ds(i, 1), :, pl.ds(core, 1)].reshape(8, 32, N)
            v = (mine.astype(F32) + r1buf[p, i].astype(F32)).astype(BF)
            acc1[p, i] = v.reshape(2, 4, 32, N)
            return 0

        lax.fori_loop(0, SEQ, one, 0)
        for j in range(1, 4):
            to_y(p, j).start()

    def carried(k, _):
        @pl.when(k > 0)
        def _():
            back_a(k).wait_recv()

        i = (s + SEQ - k) % SEQ
        cols = pl.ds(pl.multiple_of(i * Q, Q), Q)
        lead = dot(lead_s[...], pick(2, 4 * i, 4)) * RN
        S = S_buf[i]
        mixed = dot(C, S) * lead + mix[:, cols].astype(F32)
        nb[:, cols] = (nb[:, cols].astype(F32) - mixed).astype(BF)
        gs = (gb[:, cols].astype(F32) * lead).astype(BF)
        dC[...] += dot_nt(gs, S)
        return 0

    lax.fori_loop(0, SEQ, carried, 0)

    dSl = (dS[...] * RN).astype(BF)
    low[:, N:] = (dC[...] + dot(dSl, B)).astype(BF)
    product(1)
    dB[...] = dot_tn(dSl, C)
    join(1)

    def carried_back(k, _):
        @pl.when(k > 0)
        def _():
            back_g(k).wait()

        i = (s + SEQ - k) % SEQ
        cols = pl.ds(pl.multiple_of(i * Q, Q), Q)
        tail = dot(tail_s[...], pick(2, 4 * i, 4))
        G = G_buf[i]
        xs = (X[:, cols].astype(F32) * tail).astype(BF)
        dB[...] += dot_nt(xs, G)
        dx[:, cols] = (dot(B, G) * tail + dx[:, cols].astype(F32)).astype(BF)
        return 0

    lax.fori_loop(0, SEQ, carried_back, 0)
    low[:, :N] = dB[...].astype(BF)
    product(0)
    join(0)

    loads[3].wait()

    def normback(b, _):
        rows = pl.ds(pl.multiple_of(b * 128, 128), 128)
        lo = low[rows, :]
        xg = jnp.zeros((128, N), F32)
        for i in range(8):
            cols = slice(i * Q, (i + 1) * Q)
            v = dot_nt(lo, W[cols, :]) + dx[rows, cols].astype(F32)
            ng[:, cols] = v
            t = xb[rows, cols].astype(F32) * v
            xg += t[:, :N] + t[:, N : 2 * N] + t[:, 2 * N : 3 * N] + t[:, 3 * N :]
        r = r_ref[rows, :]
        back = r * r * r * (jnp.sum(xg, axis=1, keepdims=True) * (1.0 / D))
        for i in range(8):
            cols = slice(i * Q, (i + 1) * Q)
            v = r * ng[:, cols] - back * xb[rows, cols].astype(F32)
            cb[rows, cols] = (cb[rows, cols].astype(F32) + v).astype(BF)
        return 0

    lax.fori_loop(0, NB_1, normback, 0)

    for p in (1, 0):
        total = acc1[p, :, :, pl.ds(y, 1)].reshape(8, 2, 32, N).astype(F32)
        for j in range(1, 4):
            to_y(p, j).wait()
            total += r2buf[p, j - 1].astype(F32)
        acc2[:, :, :, p * N : (p + 1) * N] = total.astype(BF)

    def to_end(m):
        place, row = (side_x + m // 8) % 2, (s + m % 8) % SEQ
        return pltpu.make_async_remote_copy(
            acc2.at[row, place], r3buf.at[m - 1], u3.at[m - 1], v3.at[m - 1],
            device_id=(row, place * 8 + f % 8), device_id_type=MESH,
        )

    for m in range(1, 16):
        to_end(m).start()
    lax.fori_loop(NB_1, 4, normback, 0)
    for k in range(1, 8):
        to_peer(1, k).wait_send()
    total = acc2[pl.ds(s, 1), pl.ds(side_x, 1)].reshape(32, 256).astype(F32)
    for m in range(1, 16):
        to_end(m).wait()
        total += r3buf[m - 1].astype(F32)
    dw_ref[...] = total * (T * SEQ * FS) ** (-0.5)


def store(old_ref, grad_ref, dw_ref, old_hbm, grad_hbm, dw_hbm, sem):
    copies = []
    for p in range(4):
        rows = pl.ds(p * 128, 128)
        for n, (a, b) in enumerate(((old_ref, old_hbm), (grad_ref, grad_hbm))):
            copies.append(pltpu.make_async_copy(a.at[rows], b.at[rows], sem.at[2 * p + n]))
    copies.append(pltpu.make_async_copy(dw_ref, dw_hbm, sem.at[8]))
    for c in copies:
        c.start()
    for c in copies:
        c.wait()


def shape(*dims, dtype=BF):
    return jax.ShapeDtypeStruct(dims, dtype)


HEADS_1 = 9
HEADS_2 = 25
NB_1 = 2
VM = pl.BlockSpec(memory_space=pltpu.VMEM)
ANY = pl.BlockSpec(memory_space=pl.ANY)
DMA = pltpu.SemaphoreType.DMA
LIMIT = 52 << 20


def shards(middle, newest, middle_cot, newest_cot, log_decay, weights, gain):
    def vm(*dims, dtype=BF):
        return pltpu.VMEM(dims, dtype)

    scratch = [
        vm(T, D), vm(T, D), vm(D, T), vm(T, D), vm(D, 2 * N), vm(T, 1, dtype=F32),
        vm(T, 2 * N), vm(SEQ, N, Q), vm(SEQ, N, Q), vm(SEQ, 8, Q, dtype=F32),
        vm(T, 3 * H), vm(T, 2 * H), vm(T, 2 * H), vm(T, 2 * H),
        vm(H, T, dtype=F32), vm(H, T, dtype=F32), vm(H, T, dtype=F32),
        vm(T, T, dtype=F32), vm(T, T, dtype=F32), vm(T, D), vm(T, D),
        vm(SEQ, N, Q), vm(SEQ, N, Q), vm(SEQ, 8, Q, dtype=F32),
        vm(SEQ, N, Q), vm(SEQ, N, Q), vm(SEQ, N, Q), vm(SEQ, N, Q),
        vm(T, N, dtype=F32), vm(T, N, dtype=F32), vm(T, 2 * N), vm(128, D, dtype=F32), vm(N, T, dtype=F32),
        vm(2, 8, 8, 2, 32, N), vm(2, 8, 8, 32, N), vm(2, 8, 2, 4, 32, N), vm(2, 3, 8, 2, 32, N),
        vm(8, 2, 32, 256), vm(15, 32, 256),
        DMA((4,)), DMA((2, 8)), DMA((2, 8)), DMA((2, 8)), DMA((2, 8)),
    ] + [DMA((8,))] * 10 + [DMA((2, 8)), DMA((2, 8)), DMA((2, 3)), DMA((2, 3)), DMA((15,)), DMA((15,))]
    old, out, grad = pl.pallas_call(
        whole_step,
        name="step",
        out_shape=[vm(T, D), vm(T, D), vm(32, 2 * N, dtype=F32)],
        in_specs=[pl.BlockSpec(memory_space=pltpu.SMEM)] + [ANY] * 4 + [VM] * 2,
        out_specs=[VM, VM, VM],
        scratch_shapes=scratch,
        compiler_params=pltpu.CompilerParams(
            collective_id=0, has_side_effects=True, vmem_limit_bytes=LIMIT
        ),
    )(gain, middle[0], newest[0], middle_cot[0], newest_cot[0], log_decay[0].T, weights)
    held = [pltpu.with_memory_space_constraint(a, pltpu.VMEM) for a in (old, out, grad)]
    old, out, grad = pl.pallas_call(
        store,
        name="store",
        out_shape=[shape(T, D), shape(T, D), shape(32, 2 * N, dtype=F32)],
        in_specs=[VM] * 3,
        out_specs=[ANY] * 3,
        scratch_shapes=[DMA((9,))],
        compiler_params=pltpu.CompilerParams(vmem_limit_bytes=4 << 20),
    )(*held)
    return old[None], out[None], grad


def solution(mesh):
    return jax.shard_map(
        shards,
        mesh=mesh,
        in_specs=(P("fsdp", "seq", None),) * 5 + (P("fsdp", None), P()),
        out_specs=(P("fsdp", "seq", None), P("fsdp", "seq", None), P(("seq", "fsdp"), None)),
        check_vma=False,
    )
```
